256 devices in a mesh: tile: 64 (over y, z, core), section: 4 (over x).
Axes of the slice: x: 4, y: 4, z: 8, core: 2. Of those that a mesh axis runs over, the one named last changes fastest.
Arguments:
- features: bfloat16 [131072, 128], P(('tile', 'section')), may hold values from -6 to 6
- kernel_map: int32 [27, 131072], P(None, ('tile', 'section')), may hold values from 0 to 4096, as said below
- send_lists: int32 [64, 4, 64, 32], P('tile', 'section'), may hold values from 0 to 2048, as said below
- fine_to_coarse: int32 [131072], P('tile'), may hold values from 0 to 8191, as said below
- conv_weight: bfloat16 [27, 128, 128], replicated, may hold values from -0.125 to 0.125
- down_weight: bfloat16 [8, 128, 256], replicated, may hold values from -0.375 to 0.375
- coarse_grad: bfloat16 [65536, 256], P(('tile', 'section')), may hold values from -0.046875 to 0.046875
Outputs:
- coarse_out: bfloat16 [65536, 256], P(('tile', 'section'))
- conv_grad: float32 [27, 128, 128], replicated
- down_grad: float32 [8, 128, 256], replicated
The draws below stay inside these ranges and needn't reach their ends.
Inputs may be any that keep to these rules, and one draw needn't show every extreme that they name: Tile t sits at grid place (t % 8, (t % 32) // 8, t // 32); two different tiles are neighbours when each of their three places differs by at most 1. For sending device (p, s) and receiving tile t, the first c entries of send_lists[p, s, t] are rows of tile p (below 2048) and the rest equal 2048; c is 0 unless p is a neighbour of t, and at most 32; every device (t, s) has some neighbour sender p of its section that fills all 32. `kernel_map`: an entry below 2048 is a row of the device's own tile; an entry 2048 + p * 32 + h names a row that send_lists fills for this device from tile p; 4096 marks a missing neighbour. Entry [13, r] is row r itself. Every filled row of send_lists is named by some entry of its receiver. `fine_to_coarse`: each entry is 8 * j + o with j a coarse row of the tile (below 1024) and o an octant below 8; the entries of one tile are distinct, every coarse row of a tile has 1 to 3 fine rows, and octant 7 of the tile's last coarse row is present in every tile.
All inputs are finite; a program needn't handle non-finite values.
Results may differ from the reference program's by a relative error of at most 0.01.
Values may be sent and summed in bfloat16 or wider, within the bound.
No kernel may reach another device: no remote copies, remote signals or barrier semaphores. Data moves between devices by JAX's collectives and lax.ppermute only.
A program may use at most 64 MiB of HBM per device.

```python
import jax
import jax.numpy as jnp
from jax import lax

CHANNELS = 128
CHANNELS_OUT = 256
OFFSETS = 27
ROWS = 512
SLOTS = 32
GRID_W = 8
COARSE_ROWS = 256
TILE_ROWS = 2048
FINE = 131072
COARSE = 65536
N_TILE = 64
N_SECTION = 4


def counts_table(key):
    base_key = jax.random.fold_in(key, 11)
    first_key, second_key = jax.random.split(base_key, 2)
    least = (SLOTS + 2) // 3
    half_tiles = N_TILE // 2
    tiles = jnp.arange(N_TILE, dtype=jnp.int32)
    place_x = tiles % GRID_W
    place_y = tiles % half_tiles // GRID_W
    place_z = tiles // half_tiles
    near = jnp.abs(place_x[:, None] - place_x[None, :]) <= 1
    near = near & (jnp.abs(place_y[:, None] - place_y[None, :]) <= 1)
    near = near & (jnp.abs(place_z[:, None] - place_z[None, :]) <= 1)
    near = near & (tiles[:, None] != tiles[None, :])
    near = near[:, None, :]
    counts = jax.random.randint(first_key, (N_TILE, N_SECTION, N_TILE), least, SLOTS + 1)
    senders = tiles.reshape(1, 1, N_TILE)
    scores = jax.random.randint(second_key, (N_TILE, N_SECTION, N_TILE), 0, 1 << 20) * N_TILE + senders
    scores = jnp.where(near, scores, -1)
    full_peer = jnp.argmax(scores, axis=2).astype(jnp.int32)[..., None]
    counts = jnp.where(senders == full_peer, SLOTS, counts)
    counts = jnp.where(near, counts, 0)
    return counts.astype(jnp.int32)


def draw_send_lists(key, part):
    counts = counts_table(key)
    row_key = jax.random.fold_in(key, 12)
    row_draw = jax.random.randint(row_key, (N_TILE, N_SECTION, N_TILE, SLOTS), 0, TILE_ROWS)
    row_limit = jnp.transpose(counts, (2, 1, 0))[..., None]
    slot_ids = jnp.arange(SLOTS, dtype=jnp.int32).reshape(1, 1, 1, SLOTS)
    return jnp.where(slot_ids < row_limit, row_draw, TILE_ROWS).astype(jnp.int32)


def draw_kernel_map(key, part):
    counts = counts_table(key)
    device_total = N_TILE * N_SECTION
    flat_counts = counts.reshape(device_total, N_TILE)
    key_list = jax.random.split(jax.random.fold_in(key, 13), device_total)
    places = (OFFSETS - 1) * ROWS
    midway = (OFFSETS - 1) // 2
    pad_entry = TILE_ROWS + N_TILE * SLOTS

    def one_device(dev_key, dev_counts, dev_index):
        key_a, key_b, key_c, key_d = jax.random.split(dev_key, 4)
        slot_ids = jnp.arange(N_TILE * SLOTS, dtype=jnp.int32)
        usable = slot_ids % SLOTS < jnp.repeat(dev_counts, SLOTS)
        slot_order = jnp.argsort(jnp.where(usable, 0, 1), stable=True).astype(jnp.int32)
        usable_count = jnp.sum(usable.astype(jnp.int32))
        place_rank = jnp.argsort(jax.random.permutation(key_a, places)).astype(jnp.int32)
        category = jax.random.randint(key_b, (places,), 0, 20)
        local_rows = jax.random.randint(key_c, (places,), 0, TILE_ROWS)
        random_slot = jax.random.randint(key_d, (places,), 0, jnp.maximum(usable_count, 1))
        chosen = jnp.where(place_rank < usable_count, place_rank, random_slot)
        halo_index = TILE_ROWS + slot_order[jnp.clip(chosen, 0, N_TILE * SLOTS - 1)]
        entries = jnp.where(place_rank < usable_count, halo_index, jnp.where(category < 8, pad_entry, jnp.where(category < 15, local_rows, halo_index)))
        entries = entries.reshape(OFFSETS - 1, ROWS)
        section_pos = dev_index % N_SECTION
        centre = section_pos * ROWS + jnp.arange(ROWS, dtype=jnp.int32)
        return jnp.concatenate([entries[:midway], centre[None, :], entries[midway:]], axis=0)
    device_maps = jax.vmap(one_device)(key_list, flat_counts, jnp.arange(device_total, dtype=jnp.int32))
    return jnp.transpose(device_maps, (1, 0, 2)).reshape(OFFSETS, FINE).astype(jnp.int32)


def draw_fine_to_coarse(key, part):
    pair_count = TILE_ROWS // 4

    def one_tile(tile_key):
        key_a, key_b, key_c, key_d = jax.random.split(tile_key, 4)
        split_at = jax.random.randint(key_a, (pair_count, 1), 1, 4)
        quarter = jnp.arange(4, dtype=jnp.int32).reshape(1, 4)
        parent_local = 2 * jnp.arange(pair_count, dtype=jnp.int32).reshape(pair_count, 1) + (quarter >= split_at).astype(jnp.int32)
        scores = jax.random.randint(key_b, (pair_count, 8), 0, 1 << 20) * 8 + jnp.arange(8, dtype=jnp.int32).reshape(1, 8)
        scores = scores.at[0, 7].set(-1)
        octant_ids = jnp.argsort(scores, axis=1)[:, :4].astype(jnp.int32)
        coarse_perm = jax.random.permutation(key_c, 2 * pair_count).astype(jnp.int32)
        coarse_perm = (coarse_perm - coarse_perm[0] - 1) % (2 * pair_count)
        values = coarse_perm[parent_local] * 8 + octant_ids
        fine_perm = jax.random.permutation(key_d, TILE_ROWS)
        return values.reshape(TILE_ROWS)[fine_perm]
    key_list = jax.random.split(jax.random.fold_in(key, 14), N_TILE)
    return jax.vmap(one_tile)(key_list).reshape(FINE).astype(jnp.int32)


def level_of(key, shape, shards, smallest, top_value):
    factor_of = 1.0
    for position, shards_of in shards:
        draws = jax.random.uniform(jax.random.fold_in(jax.random.fold_in(key, 6), position), (shards_of,), jnp.float32, smallest / len(shards), top_value / len(shards))
        factor_of = factor_of * jnp.repeat(jnp.exp(draws), shape[position] // shards_of).reshape((-1,) + (1,) * (len(shape) - 1 - position))
    return factor_of


def bell_draw(rng, dims, width, bound, cuts=(), kind=jnp.bfloat16):
    values = jax.random.normal(rng, dims, jnp.float32) * width
    if len(cuts) > 0:
        values = level_of(rng, dims, cuts, -0.22, 0.18) * values
    return jnp.clip(values, min=-bound, max=bound).astype(kind)


def setup_inputs(seed: int = 0) -> dict:
    streams_of = jax.random.split(jax.random.key(seed), 8)
    features = bell_draw(streams_of[0], (FINE, CHANNELS), 1.0, 6.0, ((0, 256),))
    kernel_map = draw_kernel_map(jax.random.fold_in(streams_of[7], 71), 0)
    send_lists = draw_send_lists(jax.random.fold_in(streams_of[7], 71), 0)
    fine_to_coarse = draw_fine_to_coarse(jax.random.fold_in(streams_of[7], 71), 0)
    conv_weight = bell_draw(streams_of[4], (OFFSETS, CHANNELS, CHANNELS), (16 * CHANNELS) ** -0.5, 0.125)
    down_weight = bell_draw(streams_of[5], (8, CHANNELS, CHANNELS_OUT), (2 * CHANNELS) ** -0.5, 0.375)
    coarse_grad = bell_draw(streams_of[6], (COARSE, CHANNELS_OUT), (2.0 * COARSE ** -0.5), 0.046875, ((0, 256),))
    return dict(features=features, kernel_map=kernel_map, send_lists=send_lists, fine_to_coarse=fine_to_coarse, conv_weight=conv_weight, down_weight=down_weight, coarse_grad=coarse_grad)


def reference(features, kernel_map, send_lists, fine_to_coarse, conv_weight, down_weight, coarse_grad):
    pad_row = FINE
    padded = jnp.concatenate([features, jnp.zeros((1, CHANNELS), features.dtype)], axis=0)
    incoming = jnp.transpose(send_lists, (2, 1, 0, 3))
    sender_tile = jnp.arange(N_TILE, dtype=jnp.int32).reshape(1, 1, N_TILE, 1)
    halo_global = jnp.where(incoming < TILE_ROWS, sender_tile * TILE_ROWS + incoming, pad_row)
    halo_global = halo_global.reshape(N_TILE, N_SECTION, N_TILE * SLOTS).astype(jnp.int32)
    tile_maps = jnp.transpose(kernel_map.reshape(OFFSETS, N_TILE, N_SECTION, ROWS), (1, 0, 2, 3))
    tile_links = fine_to_coarse.reshape(N_TILE, TILE_ROWS)
    tile_grads = coarse_grad.reshape(N_TILE, N_SECTION * COARSE_ROWS, CHANNELS_OUT)
    down_flat = down_weight.reshape(8 * CHANNELS, CHANNELS_OUT)
    section_ids = jnp.arange(N_SECTION, dtype=jnp.int32).reshape(1, N_SECTION, 1)
    conv_f32 = conv_weight.astype(jnp.float32)

    def one_tile(totals, inputs):
        tile_id, tile_map, halo_map, tile_link, tile_grad = inputs
        local_row = tile_id * TILE_ROWS + tile_map
        slot_pos = jnp.clip(tile_map - TILE_ROWS, 0, N_TILE * SLOTS - 1)
        remote = halo_map[section_ids, slot_pos]
        row_index = jnp.where(tile_map < TILE_ROWS, local_row,
                              jnp.where(tile_map < TILE_ROWS + N_TILE * SLOTS, remote, pad_row))
        row_index = row_index.reshape(OFFSETS, TILE_ROWS).astype(jnp.int32)
        gathered = padded[row_index].astype(jnp.float32)
        pre_act = jnp.einsum("kic,kcd->id", gathered, conv_f32)
        hidden = jax.nn.silu(pre_act).astype(jnp.bfloat16)
        spread = jnp.zeros((N_SECTION * COARSE_ROWS * 8, CHANNELS), jnp.bfloat16).at[tile_link].set(hidden)
        spread = spread.reshape(N_SECTION * COARSE_ROWS, 8 * CHANNELS)
        coarse = jnp.dot(spread, down_flat, preferred_element_type=jnp.float32).astype(jnp.bfloat16)
        spread_grad = jnp.dot(tile_grad, down_flat.T, preferred_element_type=jnp.float32)
        hidden_grad = spread_grad.reshape(N_SECTION * COARSE_ROWS * 8, CHANNELS)[tile_link]
        gate_vals = jax.nn.sigmoid(pre_act)
        pre_grad = (hidden_grad * gate_vals * (1.0 + pre_act * (1.0 - gate_vals))).astype(jnp.bfloat16)
        conv_grad = jnp.einsum("kic,id->kcd", gathered, pre_grad.astype(jnp.float32))
        down_grad = jnp.dot(spread.T, tile_grad, preferred_element_type=jnp.float32)
        return (totals[0] + conv_grad, totals[1] + down_grad), coarse

    start = (jnp.zeros((OFFSETS, CHANNELS, CHANNELS), jnp.float32),
             jnp.zeros((8 * CHANNELS, CHANNELS_OUT), jnp.float32))
    tile_ids = jnp.arange(N_TILE, dtype=jnp.int32)
    sums, coarses = lax.scan(one_tile, start, (tile_ids, tile_maps, halo_global, tile_links, tile_grads))
    coarse_out = coarses.reshape(COARSE, CHANNELS_OUT)
    return coarse_out, sums[0], sums[1].reshape(8, CHANNELS, CHANNELS_OUT)
```

```python
import jax
import jax.numpy as jnp
from jax import lax
from jax.sharding import Mesh, PartitionSpec as P

RING_Y, DEPTH_Z, CORES, RING_X = 4, 8, 2, 4
AXES = ("y", "z", "core", "x")
TILE = ("y", "z", "core")


def device_index(place):
    tile = (place[0] * DEPTH_Z + place[1]) * CORES + place[2]
    return tile * RING_X + place[3]


def partner_pairs(partner):
    pairs = []
    for y in range(RING_Y):
        for z in range(DEPTH_Z):
            for core in range(CORES):
                for x in range(RING_X):
                    place = (y, z, core, x)
                    pairs.append((device_index(place), device_index(partner(*place))))
    return pairs


def send(value, partner):
    return lax.ppermute(value, AXES, partner_pairs(partner))


def across_core(y, z, core, x):
    return (y, z, 1 - core, x)


def first_ring(step):
    return lambda y, z, core, x: (y, z, core, x ^ step) if core == 0 else (y ^ step, z, core, x)


def second_ring(step):
    return lambda y, z, core, x: (y ^ step, z, core, x) if core == 0 else (y, z, core, x ^ step)


def along_z(step):
    return lambda y, z, core, x: (y, z ^ step, core, x)


def narrow(value):
    return value.astype(jnp.bfloat16)


def wide(value):
    return value.astype(jnp.float32)


def pick(parts, digit):
    return lax.dynamic_index_in_dim(parts, digit, 0, keepdims=False)


def scatter_pair(parts, digit, partner):
    other = send(pick(parts, 1 - digit), partner)
    return narrow(wide(pick(parts, digit)) + wide(other))


def scatter_ring(parts, digit, ring):
    received = [send(pick(parts, digit ^ step), ring(step)) for step in (1, 2, 3)]
    total = wide(pick(parts, digit))
    for part in received:
        total = total + wide(part)
    return narrow(total)


def swap(first, second, flip):
    return jnp.where(flip, second, first), jnp.where(flip, first, second)


def gather_pair(part, digit, partner):
    other = send(part, partner)
    return jnp.stack(swap(part, other, digit == 1))


def gather_ring(part, digit, ring):
    parts = [part] + [send(part, ring(step)) for step in (1, 2, 3)]
    low, high = digit % 2 == 1, digit // 2 == 1
    first, second = swap(parts[0], parts[1], low)
    third, fourth = swap(parts[2], parts[3], low)
    first, third = swap(first, third, high)
    second, fourth = swap(second, fourth, high)
    return jnp.stack([first, second, third, fourth])


def sum_over_devices(partial_sums):
    y, z, core, x = (lax.axis_index(name) for name in AXES)
    ring_one = jnp.where(core == 0, x, y)
    ring_two = jnp.where(core == 0, y, x)
    rows = partial_sums.shape[0] // (CORES * RING_X * RING_Y * 2)
    lanes = partial_sums.shape[1]
    parts = narrow(partial_sums).reshape(CORES, RING_X * RING_Y * 2 * rows, lanes)
    part = scatter_pair(parts, core, across_core)
    part = scatter_ring(part.reshape(RING_X, RING_Y * 2 * rows, lanes), ring_one, first_ring)
    part = scatter_ring(part.reshape(RING_Y, 2 * rows, lanes), ring_two, second_ring)
    part = scatter_pair(part.reshape(2, rows, lanes), z % 2, along_z(1))
    others = [send(part, along_z(step)) for step in (2, 4, 6)]
    part = narrow((wide(part) + wide(others[0])) + (wide(others[1]) + wide(others[2])))
    part = gather_pair(part, z % 2, along_z(1)).reshape(2 * rows, lanes)
    part = gather_ring(part, ring_two, second_ring).reshape(RING_Y * 2 * rows, lanes)
    part = gather_ring(part, ring_one, first_ring).reshape(RING_X * RING_Y * 2 * rows, lanes)
    return wide(gather_pair(part, core, across_core)).reshape(partial_sums.shape)


def shards(features, kernel_map, send_lists, fine_to_coarse, conv_weight, down_weight, coarse_grad):
    rows_dev, channels = features.shape
    tile_count = lax.axis_size(TILE)
    section_count = RING_X
    slot_count = send_lists.shape[-1]
    offset_count = kernel_map.shape[0]
    octants = down_weight.shape[0]
    out_channels = down_weight.shape[2]
    coarse_rows = coarse_grad.shape[0]
    coarse_tile = coarse_rows * section_count
    section_id = lax.axis_index("x")
    group_size = 9
    tile_feats = lax.all_gather(features, "x", axis=0, tiled=True)
    zero_row = jnp.zeros((1, channels), jnp.bfloat16)
    padded = jnp.concatenate([tile_feats, zero_row], axis=0)
    outgoing = padded[send_lists.reshape(tile_count, slot_count)]
    incoming = lax.all_to_all(outgoing, TILE, split_axis=0, concat_axis=0, tiled=True)
    lookup = jnp.concatenate(
        [tile_feats, incoming.reshape(tile_count * slot_count, channels), zero_row], axis=0
    )

    def gathered(group_id):
        picks = kernel_map[group_id * group_size : (group_id + 1) * group_size].T
        return lookup[picks].reshape(rows_dev, group_size * channels)

    group_total = offset_count // group_size
    pre_act = jnp.zeros((rows_dev, channels), jnp.float32)
    for group_id in range(group_total):
        weights = conv_weight[group_id * group_size : (group_id + 1) * group_size].reshape(
            group_size * channels, channels
        )
        pre_act = pre_act + jnp.dot(gathered(group_id), weights, preferred_element_type=jnp.float32)
    hidden = jax.nn.silu(pre_act).astype(jnp.bfloat16)
    own_map = lax.dynamic_slice_in_dim(fine_to_coarse, section_id * rows_dev, rows_dev)
    own_parent = own_map // octants
    own_octant = own_map % octants
    octant_hit = own_octant[:, None] == jnp.arange(octants, dtype=jnp.int32)[None, :]
    down_flat = down_weight.reshape(octants * channels, out_channels)
    tile_grad = lax.all_gather(coarse_grad, "x", axis=0, tiled=True)
    parent_grad = tile_grad[own_parent]
    stacked = jnp.transpose(down_weight, (1, 0, 2)).reshape(channels, octants * out_channels)
    every_octant = jnp.dot(hidden, stacked, preferred_element_type=jnp.float32)
    every_octant = every_octant.reshape(rows_dev, octants, out_channels)
    own_term = jnp.sum(jnp.where(octant_hit[:, :, None], every_octant, 0.0), axis=1)
    partial_value = jnp.zeros((coarse_tile, out_channels), jnp.float32).at[own_parent].add(own_term)
    coarse_out = lax.psum_scatter(
        partial_value.astype(jnp.bfloat16), "x", scatter_dimension=0, tiled=True
    )
    expanded = jnp.where(octant_hit[:, :, None], hidden[:, None, :], jnp.zeros((), jnp.bfloat16))
    expanded = expanded.reshape(rows_dev, octants * channels)
    down_grad = lax.dot_general(
        expanded, parent_grad, (((0,), (0,)), ((), ())), preferred_element_type=jnp.float32
    )
    back_all = lax.dot_general(
        parent_grad, down_flat, (((1,), (1,)), ((), ())), preferred_element_type=jnp.float32
    )
    back_all = back_all.reshape(rows_dev, octants, channels)
    hidden_grad = jnp.sum(jnp.where(octant_hit[:, :, None], back_all, 0.0), axis=1)
    gate_vals = jax.nn.sigmoid(pre_act)
    pre_grad = (hidden_grad * gate_vals * (1.0 + pre_act * (1.0 - gate_vals))).astype(jnp.bfloat16)
    conv_parts = []
    for group_id in range(group_total):
        product = lax.dot_general(
            gathered(group_id),
            pre_grad,
            (((0,), (0,)), ((), ())),
            preferred_element_type=jnp.float32,
        )
        conv_parts.append(product.reshape(group_size, channels, channels))
    conv_grad = jnp.concatenate(conv_parts, axis=0)
    conv_flat = conv_grad.reshape(offset_count * channels, channels)
    down_flat = jnp.concatenate([down_grad[:, :channels], down_grad[:, channels:]], axis=0)
    used = conv_flat.shape[0] + down_flat.shape[0]
    filler = jnp.zeros((-used % 512, channels), jnp.float32)
    sums = sum_over_devices(jnp.concatenate([conv_flat, down_flat, filler], axis=0))
    conv_grad = sums[: conv_flat.shape[0]].reshape(offset_count, channels, channels)
    down_sums = sums[conv_flat.shape[0] : used]
    half = octants * channels
    down_grad = jnp.concatenate([down_sums[:half], down_sums[half:]], axis=1)
    down_grad = down_grad.reshape(octants, channels, out_channels)
    return (coarse_out, conv_grad, down_grad)


def solution(mesh):
    fine_mesh = Mesh(mesh.devices.reshape(RING_Y, DEPTH_Z, CORES, RING_X), AXES)
    placed = (
        P(AXES, None),
        P(None, AXES),
        P(TILE, "x", None, None),
        P(TILE),
        P(),
        P(),
        P(AXES, None),
    )
    return jax.shard_map(
        shards,
        mesh=fine_mesh,
        in_specs=placed,
        out_specs=(P(AXES, None), P(), P()),
        check_vma=False,
    )
```

```python
import jax
import jax.numpy as jnp
from jax import lax
from jax.experimental import pallas as pl
from jax.experimental.pallas import tpu as pltpu
from jax.sharding import Mesh, PartitionSpec as P

RING_Y, DEPTH_Z, CORES, RING_X = 4, 8, 2, 4
AXES = ("y", "z", "core", "x")
TILE = ("y", "z", "core")
UNROLL = 16


def device_index(place):
    tile = (place[0] * DEPTH_Z + place[1]) * CORES + place[2]
    return tile * RING_X + place[3]


def partner_pairs(partner):
    pairs = []
    for y in range(RING_Y):
        for z in range(DEPTH_Z):
            for core in range(CORES):
                for x in range(RING_X):
                    place = (y, z, core, x)
                    pairs.append((device_index(place), device_index(partner(*place))))
    return pairs


def send(value, partner):
    return lax.ppermute(value, AXES, partner_pairs(partner))


def across_core(y, z, core, x):
    return (y, z, 1 - core, x)


def first_ring(step):
    return lambda y, z, core, x: (y, z, core, x ^ step) if core == 0 else (y ^ step, z, core, x)


def second_ring(step):
    return lambda y, z, core, x: (y ^ step, z, core, x) if core == 0 else (y, z, core, x ^ step)


def along_z(step):
    return lambda y, z, core, x: (y, z ^ step, core, x)


def narrow(value):
    return value.astype(jnp.bfloat16)


def wide(value):
    return value.astype(jnp.float32)


def pick(parts, digit):
    return lax.dynamic_index_in_dim(parts, digit, 0, keepdims=False)


def scatter_pair(parts, digit, partner):
    other = send(pick(parts, 1 - digit), partner)
    return narrow(wide(pick(parts, digit)) + wide(other))


def scatter_ring(parts, digit, ring):
    received = [send(pick(parts, digit ^ step), ring(step)) for step in (1, 2, 3)]
    total = wide(pick(parts, digit))
    for part in received:
        total = total + wide(part)
    return narrow(total)


def swap(first, second, flip):
    return jnp.where(flip, second, first), jnp.where(flip, first, second)


def gather_pair(part, digit, partner):
    other = send(part, partner)
    return jnp.stack(swap(part, other, digit == 1))


def gather_ring(part, digit, ring):
    parts = [part] + [send(part, ring(step)) for step in (1, 2, 3)]
    low, high = digit % 2 == 1, digit // 2 == 1
    first, second = swap(parts[0], parts[1], low)
    third, fourth = swap(parts[2], parts[3], low)
    first, third = swap(first, third, high)
    second, fourth = swap(second, fourth, high)
    return jnp.stack([first, second, third, fourth])


def sum_over_devices(partial_sums, coarse):
    y, z, core, x = (lax.axis_index(name) for name in AXES)
    ring_one = jnp.where(core == 0, x, y)
    ring_two = jnp.where(core == 0, y, x)
    rows = partial_sums.shape[0] // (CORES * RING_X * RING_Y * 2)
    lanes = partial_sums.shape[1]
    parts = partial_sums.reshape(CORES, RING_X * RING_Y * 2 * rows, lanes)
    part = scatter_pair(parts, core, across_core)
    part = scatter_ring(part.reshape(RING_X, RING_Y * 2 * rows, lanes), ring_one, first_ring)
    part, coarse = lax.optimization_barrier((part, coarse))
    part = scatter_ring(part.reshape(RING_Y, 2 * rows, lanes), ring_two, second_ring)
    part = scatter_pair(part.reshape(2, rows, lanes), z % 2, along_z(1))
    others = [send(part, along_z(step)) for step in (2, 4, 6)]
    part = narrow((wide(part) + wide(others[0])) + (wide(others[1]) + wide(others[2])))
    part = gather_pair(part, z % 2, along_z(1)).reshape(2 * rows, lanes)
    part = gather_ring(part, ring_two, second_ring).reshape(RING_Y * 2 * rows, lanes)
    part = gather_ring(part, ring_one, first_ring).reshape(RING_X * RING_Y * 2 * rows, lanes)
    return wide(gather_pair(part, core, across_core)).reshape(partial_sums.shape), coarse


def ring_x(step):
    return lambda y, z, core, x: (y, z, core, x ^ step)


def share_over_x(value):
    return [value] + [send(value, ring_x(step)) for step in (1, 2, 3)]


def place_parts(target, parts, x):
    rows = parts[0].shape[0]
    for step, part in enumerate(parts):
        start = pl.multiple_of((x ^ step) * rows, rows)
        target[pl.ds(start, rows), :] = part[...].astype(target.dtype)


def copy_rows(table, target, picks, count):
    def block(block_id, carry):
        base = pl.multiple_of(block_id * UNROLL, UNROLL)
        rows = [table[pl.ds(picks(base + j), 1), :] for j in range(UNROLL)]
        for j, row in enumerate(rows):
            target[pl.ds(base + j, 1), :] = row
        return carry

    lax.fori_loop(0, count // UNROLL, block, 0)


def pick_halo(lists, part0, part1, part2, part3, out, table, stage):
    tile_rows = 4 * part0.shape[0]
    slots = lists.shape[1]
    place_parts(table, (part0, part1, part2, part3), lax.axis_index("x"))
    table[pl.ds(tile_rows, 8), :] = jnp.zeros((8, table.shape[1]), jnp.float32)
    copy_rows(table, stage, lambda at: lists[at // slots, at % slots], stage.shape[0])
    out[...] = stage[...].astype(jnp.bfloat16)


def matmul(left, right, left_dim=1, right_dim=0):
    return lax.dot_general(
        left, right, (((left_dim,), (right_dim,)), ((), ())), preferred_element_type=jnp.float32
    )


def step_kernel(
    kernel_map, part0, part1, part2, part3, incoming, conv_weight, down_weight,
    grad0, grad1, grad2, grad3, link_column, link_row,
    coarse, sums, table, stage, gathered, pre_act, tile_grad,
):
    x = lax.axis_index("x")
    offsets, rows = kernel_map.shape
    channels = part0.shape[1]
    octants, _, out_channels = down_weight.shape
    tile_rows = 4 * rows
    coarse_tile = tile_grad.shape[0]
    place_parts(table, (part0, part1, part2, part3), x)
    table[pl.ds(tile_rows, incoming.shape[0]), :] = incoming[...].astype(jnp.float32)
    table[pl.ds(tile_rows + incoming.shape[0], 8), :] = jnp.zeros((8, channels), jnp.float32)
    place_parts(tile_grad, (grad0, grad1, grad2, grad3), x)
    pre_act[...] = jnp.zeros_like(pre_act)

    def forward(offset, carry):
        copy_rows(table, stage, lambda at: kernel_map[offset, at], rows)
        block = stage[...].astype(jnp.bfloat16)
        gathered[offset] = block
        pre_act[...] += matmul(block, conv_weight[offset])
        return carry

    lax.fori_loop(0, offsets, forward, 0)

    act = pre_act[...]
    gate = 1.0 / (1.0 + jnp.exp(-act))
    hidden = (act * gate).astype(jnp.bfloat16)
    link = link_column[...]
    octant = link % octants
    at_parent = (link // octants) == lax.broadcasted_iota(jnp.int32, (rows, coarse_tile), 1)
    parent_grad = matmul(at_parent.astype(jnp.bfloat16), tile_grad[...]).astype(jnp.bfloat16)
    own_term = jnp.zeros((rows, out_channels), jnp.float32)
    hidden_grad = jnp.zeros((rows, channels), jnp.float32)
    conv_rows = offsets * channels
    for o in range(octants):
        hit = octant == o
        weight = down_weight[o]
        only = jnp.where(hit, hidden, jnp.zeros_like(hidden))
        own_term += matmul(only, weight)
        product = matmul(only, parent_grad, 0, 0).astype(jnp.bfloat16)
        sums[pl.ds(conv_rows + o * channels, channels), :] = product[:, :channels]
        sums[pl.ds(conv_rows + (octants + o) * channels, channels), :] = product[:, channels:]
        hidden_grad += jnp.where(hit, matmul(parent_grad, weight, 1, 1), 0.0)
    pre_grad = (hidden_grad * gate * (1.0 + act * (1.0 - gate))).astype(jnp.bfloat16)

    from_row = (link_row[...] // octants) == lax.broadcasted_iota(jnp.int32, (coarse_tile, rows), 0)
    from_row = from_row.astype(jnp.bfloat16)
    high = own_term.astype(jnp.bfloat16)
    low = (own_term - high.astype(jnp.float32)).astype(jnp.bfloat16)
    coarse[...] = (matmul(from_row, high) + matmul(from_row, low)).astype(jnp.bfloat16)

    def backward(offset, carry):
        start = pl.multiple_of(offset * channels, channels)
        product = matmul(gathered[offset], pre_grad, 0, 0)
        sums[pl.ds(start, channels), :] = product.astype(jnp.bfloat16)
        return carry

    lax.fori_loop(0, offsets, backward, 0)
    used = conv_rows + 2 * octants * channels
    sums[pl.ds(used, sums.shape[0] - used), :] = jnp.zeros((sums.shape[0] - used, channels), jnp.bfloat16)


def shards(features, kernel_map, send_lists, fine_to_coarse, conv_weight, down_weight, coarse_grad):
    rows, channels = features.shape
    tiles, slots = send_lists.shape[2:]
    offsets = kernel_map.shape[0]
    octants, _, out_channels = down_weight.shape
    tile_rows = RING_X * rows
    coarse_rows = coarse_grad.shape[0]
    coarse_tile = RING_X * coarse_rows
    x = lax.axis_index("x")
    smem, vmem = pl.BlockSpec(memory_space=pltpu.SMEM), pl.BlockSpec(memory_space=pltpu.VMEM)
    parts = share_over_x(features)
    outgoing = pl.pallas_call(
        pick_halo,
        out_shape=jax.ShapeDtypeStruct((tiles * slots, channels), jnp.bfloat16),
        in_specs=[smem] + [vmem] * 4,
        out_specs=vmem,
        scratch_shapes=[
            pltpu.VMEM((tile_rows + 8, channels), jnp.float32),
            pltpu.VMEM((tiles * slots, channels), jnp.float32),
        ],
        compiler_params=pltpu.CompilerParams(vmem_limit_bytes=16 << 20),
        name="pick_halo",
    )(send_lists.reshape(tiles, slots), *parts)
    later_grad, outgoing = lax.optimization_barrier((coarse_grad, outgoing))
    incoming = lax.all_to_all(
        outgoing.reshape(tiles, slots, channels), TILE, split_axis=0, concat_axis=0, tiled=True
    )
    grads = share_over_x(later_grad)
    link = lax.dynamic_slice_in_dim(fine_to_coarse, x * rows, rows)
    used = offsets * channels + 2 * octants * channels
    total = used + (-used % 512)
    coarse, sums = pl.pallas_call(
        step_kernel,
        out_shape=(
            jax.ShapeDtypeStruct((coarse_tile, out_channels), jnp.bfloat16),
            jax.ShapeDtypeStruct((total, channels), jnp.bfloat16),
        ),
        in_specs=[smem] + [vmem] * 13,
        out_specs=(vmem, vmem),
        scratch_shapes=[
            pltpu.VMEM((tile_rows + tiles * slots + 8, channels), jnp.float32),
            pltpu.VMEM((rows, channels), jnp.float32),
            pltpu.VMEM((offsets, rows, channels), jnp.bfloat16),
            pltpu.VMEM((rows, channels), jnp.float32),
            pltpu.VMEM((coarse_tile, out_channels), jnp.bfloat16),
        ],
        compiler_params=pltpu.CompilerParams(vmem_limit_bytes=40 << 20),
        name="step",
    )(
        kernel_map, *parts, incoming.reshape(tiles * slots, channels), conv_weight, down_weight,
        *grads, link.reshape(rows, 1), link.reshape(1, rows),
    )
    sums, coarse = sum_over_devices(sums, coarse)
    coarse = coarse.reshape(RING_X, coarse_rows, out_channels)
    shares = [wide(pick(coarse, x))]
    shares += [wide(send(pick(coarse, x ^ step), ring_x(step))) for step in (1, 2, 3)]
    coarse_out = narrow((shares[0] + shares[1]) + (shares[2] + shares[3]))
    conv_grad = sums[: offsets * channels].reshape(offsets, channels, channels)
    down_sums = sums[offsets * channels : used]
    half = octants * channels
    down_grad = jnp.concatenate([down_sums[:half], down_sums[half:]], axis=1)
    down_grad = down_grad.reshape(octants, channels, out_channels)
    return (coarse_out, conv_grad, down_grad)


def solution(mesh):
    fine_mesh = Mesh(mesh.devices.reshape(RING_Y, DEPTH_Z, CORES, RING_X), AXES)
    placed = (
        P(AXES, None),
        P(None, AXES),
        P(TILE, "x", None, None),
        P(TILE),
        P(),
        P(),
        P(AXES, None),
    )
    return jax.shard_map(
        shards,
        mesh=fine_mesh,
        in_specs=placed,
        out_specs=(P(AXES, None), P(), P()),
        check_vma=False,
    )
```

```python
import jax
import jax.numpy as jnp
from jax import lax
from jax.experimental import pallas as pl
from jax.experimental.pallas import tpu as pltpu
from jax.sharding import Mesh, PartitionSpec as P

RING_Y, DEPTH_Z, CORES, RING_X = 4, 8, 2, 4
AXES = ("y", "z", "core", "x")
TILE = ("y", "z", "core")
UNROLL = 32


def device_index(place):
    tile = (place[0] * DEPTH_Z + place[1]) * CORES + place[2]
    return tile * RING_X + place[3]


def partner_pairs(partner):
    pairs = []
    for y in range(RING_Y):
        for z in range(DEPTH_Z):
            for core in range(CORES):
                for x in range(RING_X):
                    place = (y, z, core, x)
                    pairs.append((device_index(place), device_index(partner(*place))))
    return pairs


def send(value, partner):
    return lax.ppermute(value, AXES, partner_pairs(partner))


def across_core(y, z, core, x):
    return (y, z, 1 - core, x)


def first_ring(step):
    return lambda y, z, core, x: (y, z, core, x ^ step) if core == 0 else (y ^ step, z, core, x)


def second_ring(step):
    return lambda y, z, core, x: (y ^ step, z, core, x) if core == 0 else (y, z, core, x ^ step)


def along_z(step):
    return lambda y, z, core, x: (y, z ^ step, core, x)


def narrow(value):
    return value.astype(jnp.bfloat16)


def wide(value):
    return value.astype(jnp.float32)


def pick(parts, digit):
    return lax.dynamic_index_in_dim(parts, digit, 0, keepdims=False)


def scatter_pair(parts, digit, partner):
    other = send(pick(parts, 1 - digit), partner)
    return narrow(wide(pick(parts, digit)) + wide(other))


def scatter_ring(parts, digit, ring):
    received = [send(pick(parts, digit ^ step), ring(step)) for step in (1, 2, 3)]
    total = wide(pick(parts, digit))
    for part in received:
        total = total + wide(part)
    return narrow(total)


def swap(first, second, flip):
    return jnp.where(flip, second, first), jnp.where(flip, first, second)


def gather_pair(part, digit, partner):
    other = send(part, partner)
    return jnp.stack(swap(part, other, digit == 1))


def gather_ring(part, digit, ring):
    parts = [part] + [send(part, ring(step)) for step in (1, 2, 3)]
    low, high = digit % 2 == 1, digit // 2 == 1
    first, second = swap(parts[0], parts[1], low)
    third, fourth = swap(parts[2], parts[3], low)
    first, third = swap(first, third, high)
    second, fourth = swap(second, fourth, high)
    return jnp.stack([first, second, third, fourth])


def sum_over_devices(partial_sums, coarse):
    y, z, core, x = (lax.axis_index(name) for name in AXES)
    ring_one = jnp.where(core == 0, x, y)
    ring_two = jnp.where(core == 0, y, x)
    rows = partial_sums.shape[0] // (CORES * RING_X * RING_Y * 2)
    lanes = partial_sums.shape[1]
    parts = partial_sums.reshape(CORES, RING_X * RING_Y * 2 * rows, lanes)
    part = scatter_pair(parts, core, across_core)
    part = scatter_ring(part.reshape(RING_X, RING_Y * 2 * rows, lanes), ring_one, first_ring)
    part, coarse = lax.optimization_barrier((part, coarse))
    shares = coarse.reshape(RING_X, coarse.shape[0] // RING_X, coarse.shape[1])
    shares = lax.all_to_all(shares, "x", split_axis=0, concat_axis=0, tiled=True)
    coarse_out = narrow(jnp.sum(wide(shares), axis=0))
    part = scatter_ring(part.reshape(RING_Y, 2 * rows, lanes), ring_two, second_ring)
    part = scatter_pair(part.reshape(2, rows, lanes), z % 2, along_z(1))
    part, coarse_out = lax.optimization_barrier((part, coarse_out))
    others = [send(part, along_z(step)) for step in (2, 4, 6)]
    part = narrow((wide(part) + wide(others[0])) + (wide(others[1]) + wide(others[2])))
    part = gather_pair(part, z % 2, along_z(1)).reshape(2 * rows, lanes)
    part = gather_ring(part, ring_two, second_ring).reshape(RING_Y * 2 * rows, lanes)
    part = gather_ring(part, ring_one, first_ring).reshape(RING_X * RING_Y * 2 * rows, lanes)
    return wide(gather_pair(part, core, across_core)).reshape(partial_sums.shape), coarse_out


def ring_x(step):
    return lambda y, z, core, x: (y, z, core, x ^ step)


def share_over_x(value):
    return [value] + [send(value, ring_x(step)) for step in (1, 2, 3)]


def part_copies(parts, target, sems, first):
    x = lax.axis_index("x")
    rows = parts[0].shape[0]
    copies = []
    for step, part in enumerate(parts):
        place = target.at[pl.ds(pl.multiple_of((x ^ step) * rows, rows), rows)]
        copies.append(pltpu.make_async_copy(part, place, sems.at[first + step]))
    return copies


def copy_rows(table, target, picks, first, count):
    for start in range(0, count, UNROLL):
        places = range(start, min(start + UNROLL, count))
        rows = [table[pl.ds(picks[first + at], 1), :] for at in places]
        for at, row in zip(places, rows):
            target[at : at + 1, :] = row


def matmul(left, right, left_dim=1, right_dim=0):
    return lax.dot_general(
        left, right, (((left_dim,), (right_dim,)), ((), ())), preferred_element_type=jnp.float32
    )


def pick_halo(lists, part0, part1, part2, part3, out, tile_feats, table, stage, sems):
    tile_rows, channels = tile_feats.shape
    block = stage.shape[0]
    copies = part_copies((part0, part1, part2, part3), tile_feats, sems, 0)
    for copy in copies:
        copy.start()
    table[pl.ds(tile_rows, 8), :] = jnp.zeros((8, channels), jnp.float32)
    for copy in copies:
        copy.wait()
    table[pl.ds(0, tile_rows), :] = tile_feats[...].astype(jnp.float32)

    def body(block_id, carry):
        first = pl.multiple_of(block_id * block, block)
        copy_rows(table, stage, lists, first, block)
        out[pl.ds(first, block), :] = stage[...].astype(jnp.bfloat16)
        return carry

    lax.fori_loop(0, out.shape[0] // block, body, 0)


def step_kernel(
    kernel_map, part0, part1, part2, part3, incoming, conv_hbm, down_hbm,
    grad0, grad1, grad2, grad3, link_column, link_row,
    coarse, sums,
    tile_feats, halo_feats, table, stage, gathered, pre_act, conv_weight, down_weight, tile_grad, sems,
):
    rows, channels = part0.shape
    offsets = conv_weight.shape[0]
    octants, _, out_channels = down_weight.shape
    tile_rows, halo_rows = tile_feats.shape[0], halo_feats.shape[0]
    coarse_tile = tile_grad.shape[0]
    feats = part_copies((part0, part1, part2, part3), tile_feats, sems, 0)
    halo = pltpu.make_async_copy(incoming, halo_feats, sems.at[4])
    conv = pltpu.make_async_copy(conv_hbm, conv_weight, sems.at[5])
    down = pltpu.make_async_copy(down_hbm, down_weight, sems.at[6])
    grads = part_copies((grad0, grad1, grad2, grad3), tile_grad, sems, 7)
    for copy in feats + [halo, conv, down] + grads:
        copy.start()
    pre_act[...] = jnp.zeros_like(pre_act)
    table[pl.ds(tile_rows + halo_rows, 8), :] = jnp.zeros((8, channels), jnp.float32)
    for copy in feats:
        copy.wait()
    table[pl.ds(0, tile_rows), :] = tile_feats[...].astype(jnp.float32)
    middle = offsets // 2
    own = pl.multiple_of(lax.axis_index("x") * rows, rows)
    gathered[middle] = tile_feats[pl.ds(own, rows), :]
    halo.wait()
    table[pl.ds(tile_rows, halo_rows), :] = halo_feats[...].astype(jnp.float32)
    conv.wait()

    def forward(at, previous):
        offset = at + (at >= middle).astype(jnp.int32)
        pre_act[...] += matmul(gathered[previous], conv_weight[previous])
        copy_rows(table, stage, kernel_map, offset * rows, rows)
        gathered[offset] = stage[...].astype(jnp.bfloat16)
        return offset

    last = lax.fori_loop(0, offsets - 1, forward, jnp.int32(middle))
    pre_act[...] += matmul(gathered[last], conv_weight[last])

    act = pre_act[...]
    gate = 1.0 / (1.0 + jnp.exp(-act))
    hidden_wide = act * gate
    hidden = hidden_wide.astype(jnp.bfloat16)
    hidden_turned = hidden_wide.T.astype(jnp.bfloat16)
    link = link_column[...]
    octant = link % octants
    link_turned = link_row[...]
    octant_turned = link_turned % octants
    at_parent = (link // octants) == lax.broadcasted_iota(jnp.int32, (rows, coarse_tile), 1)
    for copy in [down] + grads:
        copy.wait()
    parent_grad = matmul(at_parent.astype(jnp.bfloat16), tile_grad[...]).astype(jnp.bfloat16)
    own_term = jnp.zeros((rows, out_channels), jnp.float32)
    hidden_grad = jnp.zeros((rows, channels), jnp.float32)
    conv_rows = offsets * channels
    for o in range(octants):
        hit = octant == o
        weight = down_weight[o]
        own_term += matmul(jnp.where(hit, hidden, jnp.zeros_like(hidden)), weight)
        hidden_grad += jnp.where(hit, matmul(parent_grad, weight, 1, 1), 0.0)
        only = jnp.where(octant_turned == o, hidden_turned, jnp.zeros_like(hidden_turned))
        product = matmul(only, parent_grad).astype(jnp.bfloat16)
        sums[pl.ds(conv_rows + o * channels, channels), :] = product[:, :channels]
        sums[pl.ds(conv_rows + (octants + o) * channels, channels), :] = product[:, channels:]
    pre_grad = hidden_grad * gate * (1.0 + act * (1.0 - gate))
    pre_grad_turned = pre_grad.T.astype(jnp.bfloat16)

    from_row = (link_turned // octants) == lax.broadcasted_iota(jnp.int32, (coarse_tile, rows), 0)
    from_row = from_row.astype(jnp.bfloat16)
    high = own_term.astype(jnp.bfloat16)
    low = (own_term - high.astype(jnp.float32)).astype(jnp.bfloat16)
    coarse[...] = (matmul(from_row, high) + matmul(from_row, low)).astype(jnp.bfloat16)

    def backward(offset, carry):
        start = pl.multiple_of(offset * channels, channels)
        turned = matmul(pre_grad_turned, gathered[offset])
        sums[pl.ds(start, channels), :] = turned.T.astype(jnp.bfloat16)
        return carry

    lax.fori_loop(0, offsets, backward, 0, unroll=3)
    used = conv_rows + 2 * octants * channels
    sums[pl.ds(used, sums.shape[0] - used), :] = jnp.zeros((sums.shape[0] - used, channels), jnp.bfloat16)


def shards(features, kernel_map, send_lists, fine_to_coarse, conv_weight, down_weight, coarse_grad):
    rows, channels = features.shape
    tiles, slots = send_lists.shape[2:]
    offsets = kernel_map.shape[0]
    octants, _, out_channels = down_weight.shape
    tile_rows, halo_rows = RING_X * rows, tiles * slots
    coarse_rows = coarse_grad.shape[0]
    coarse_tile = RING_X * coarse_rows
    smem, vmem = pl.BlockSpec(memory_space=pltpu.SMEM), pl.BlockSpec(memory_space=pltpu.VMEM)
    anywhere = pl.BlockSpec(memory_space=pl.ANY)
    parts = share_over_x(features)
    outgoing = pl.pallas_call(
        pick_halo,
        out_shape=jax.ShapeDtypeStruct((halo_rows, channels), jnp.bfloat16),
        in_specs=[smem] + [anywhere] * 4,
        out_specs=vmem,
        scratch_shapes=[
            pltpu.VMEM((tile_rows, channels), jnp.bfloat16),
            pltpu.VMEM((tile_rows + 8, channels), jnp.float32),
            pltpu.VMEM((128, channels), jnp.float32),
            pltpu.SemaphoreType.DMA((4,)),
        ],
        compiler_params=pltpu.CompilerParams(vmem_limit_bytes=16 << 20),
        name="pick_halo",
    )(send_lists.reshape(halo_rows), *parts)
    later_grad, outgoing = lax.optimization_barrier((coarse_grad, outgoing))
    incoming = lax.all_to_all(
        outgoing.reshape(tiles, slots, channels), TILE, split_axis=0, concat_axis=0, tiled=True
    )
    grads = share_over_x(later_grad)
    x = lax.axis_index("x")
    link = lax.dynamic_slice_in_dim(fine_to_coarse, x * rows, rows)
    used = offsets * channels + 2 * octants * channels
    total = used + (-used % 512)
    coarse, sums = pl.pallas_call(
        step_kernel,
        out_shape=(
            jax.ShapeDtypeStruct((coarse_tile, out_channels), jnp.bfloat16),
            jax.ShapeDtypeStruct((total, channels), jnp.bfloat16),
        ),
        in_specs=[smem] + [anywhere] * 11 + [vmem] * 2,
        out_specs=(vmem, vmem),
        scratch_shapes=[
            pltpu.VMEM((tile_rows, channels), jnp.bfloat16),
            pltpu.VMEM((halo_rows, channels), jnp.bfloat16),
            pltpu.VMEM((tile_rows + halo_rows + 8, channels), jnp.float32),
            pltpu.VMEM((rows, channels), jnp.float32),
            pltpu.VMEM((offsets, rows, channels), jnp.bfloat16),
            pltpu.VMEM((rows, channels), jnp.float32),
            pltpu.VMEM(conv_weight.shape, jnp.bfloat16),
            pltpu.VMEM(down_weight.shape, jnp.bfloat16),
            pltpu.VMEM((coarse_tile, out_channels), jnp.bfloat16),
            pltpu.SemaphoreType.DMA((11,)),
        ],
        compiler_params=pltpu.CompilerParams(vmem_limit_bytes=40 << 20),
        name="step",
    )(
        kernel_map.reshape(offsets * rows), *parts, incoming.reshape(halo_rows, channels),
        conv_weight, down_weight, *grads, link.reshape(rows, 1), link.reshape(1, rows),
    )
    sums, coarse_out = sum_over_devices(sums, coarse)
    conv_grad = sums[: offsets * channels].reshape(offsets, channels, channels)
    down_sums = sums[offsets * channels : used]
    half = octants * channels
    down_grad = jnp.concatenate([down_sums[:half], down_sums[half:]], axis=1)
    down_grad = down_grad.reshape(octants, channels, out_channels)
    return (coarse_out, conv_grad, down_grad)


def solution(mesh):
    fine_mesh = Mesh(mesh.devices.reshape(RING_Y, DEPTH_Z, CORES, RING_X), AXES)
    placed = (
        P(AXES, None),
        P(None, AXES),
        P(TILE, "x", None, None),
        P(TILE),
        P(),
        P(),
        P(AXES, None),
    )
    return jax.shard_map(
        shards,
        mesh=fine_mesh,
        in_specs=placed,
        out_specs=(P(AXES, None), P(), P()),
        check_vma=False,
    )
```

```python
import jax
import jax.numpy as jnp
from jax import lax
from jax.experimental import pallas as pl
from jax.experimental.pallas import tpu as pltpu
from jax.sharding import Mesh, PartitionSpec as P

RING_Y, DEPTH_Z, CORES, RING_X = 4, 8, 2, 4
AXES = ("y", "z", "core", "x")
TILE = ("y", "z", "core")
UNROLL = 32


def device_index(place):
    tile = (place[0] * DEPTH_Z + place[1]) * CORES + place[2]
    return tile * RING_X + place[3]


def partner_pairs(partner):
    pairs = []
    for y in range(RING_Y):
        for z in range(DEPTH_Z):
            for core in range(CORES):
                for x in range(RING_X):
                    place = (y, z, core, x)
                    pairs.append((device_index(place), device_index(partner(*place))))
    return pairs


def send(value, partner):
    return lax.ppermute(value, AXES, partner_pairs(partner))


def across_core(y, z, core, x):
    return (y, z, 1 - core, x)


def square(step, hop):
    def partner(y, z, core, x):
        return (y ^ (hop if step & 2 else 0), z, core, x ^ (hop if step & 1 else 0))

    return partner


def first_ring(step):
    return lambda y, z, core, x: square(step, 3 if core else 1)(y, z, core, x)


def second_ring(step):
    return lambda y, z, core, x: square(step, 1 if core else 3)(y, z, core, x)


def along_z(step):
    return lambda y, z, core, x: (y, z ^ step, core, x)


def narrow(value):
    return value.astype(jnp.bfloat16)


def wide(value):
    return value.astype(jnp.float32)


def pick(parts, digit):
    return lax.dynamic_index_in_dim(parts, digit, 0, keepdims=False)


def scatter_pair(parts, digit, partner):
    other = send(pick(parts, 1 - digit), partner)
    return narrow(wide(pick(parts, digit)) + wide(other))


def scatter_ring(parts, digit, ring):
    received = [send(pick(parts, digit ^ step), ring(step)) for step in (1, 2, 3)]
    total = wide(pick(parts, digit))
    for part in received:
        total = total + wide(part)
    return narrow(total)


def swap(first, second, flip):
    return jnp.where(flip, second, first), jnp.where(flip, first, second)


def gather_pair(part, digit, partner):
    other = send(part, partner)
    return jnp.stack(swap(part, other, digit == 1))


def gather_ring(part, digit, ring):
    parts = [part] + [send(part, ring(step)) for step in (1, 2, 3)]
    low, high = digit % 2 == 1, digit // 2 == 1
    first, second = swap(parts[0], parts[1], low)
    third, fourth = swap(parts[2], parts[3], low)
    first, third = swap(first, third, high)
    second, fourth = swap(second, fourth, high)
    return jnp.stack([first, second, third, fourth])


def sum_over_devices(partial_sums, coarse):
    y, z, core, x = (lax.axis_index(name) for name in AXES)
    near_x, near_y = (x ^ (x >> 1)) & 1, (y ^ (y >> 1)) & 1
    far_x, far_y = x >> 1, y >> 1
    near, far = near_x + 2 * near_y, far_x + 2 * far_y
    ring_one = jnp.where(core == 0, near, far)
    ring_two = jnp.where(core == 0, far, near)
    rows = partial_sums.shape[0] // (CORES * RING_X * RING_Y)
    lanes = partial_sums.shape[1]
    parts = partial_sums.reshape(CORES, RING_X * RING_Y * rows, lanes)
    part = scatter_pair(parts, core, across_core)
    part = scatter_ring(part.reshape(RING_X, RING_Y * rows, lanes), ring_one, first_ring)
    part, coarse = lax.optimization_barrier((part, coarse))
    shares = coarse.reshape(RING_X, coarse.shape[0] // RING_X, coarse.shape[1])
    shares = lax.all_to_all(shares, "x", split_axis=0, concat_axis=0, tiled=True)
    coarse_out = narrow(jnp.sum(wide(shares), axis=0))
    part = scatter_ring(part.reshape(RING_Y, rows, lanes), ring_two, second_ring)
    for step in (1, 2, 7):
        part = narrow(wide(part) + wide(send(part, along_z(step))))
    part = gather_ring(part, ring_two, second_ring).reshape(RING_Y * rows, lanes)
    part = gather_ring(part, ring_one, first_ring).reshape(RING_X * RING_Y * rows, lanes)
    return wide(gather_pair(part, core, across_core)).reshape(partial_sums.shape), coarse_out


def ring_x(step):
    return lambda y, z, core, x: (y, z, core, x ^ step)


def share_over_x(value):
    return [value] + [send(value, ring_x(step)) for step in (1, 2, 3)]


def part_copies(parts, target, sems, first):
    x = lax.axis_index("x")
    rows = parts[0].shape[0]
    copies = []
    for step, part in enumerate(parts):
        place = target.at[pl.ds(pl.multiple_of((x ^ step) * rows, rows), rows)]
        copies.append(pltpu.make_async_copy(part, place, sems.at[first + step]))
    return copies


def copy_rows(table, target, picks, first, count):
    for start in range(0, count, UNROLL):
        places = range(start, min(start + UNROLL, count))
        rows = [table[pl.ds(picks[first + at], 1), :] for at in places]
        for at, row in zip(places, rows):
            target[at : at + 1, :] = row


def matmul(left, right, left_dim=1, right_dim=0):
    return lax.dot_general(
        left, right, (((left_dim,), (right_dim,)), ((), ())), preferred_element_type=jnp.float32
    )


def pick_halo(lists, part0, part1, part2, part3, out, tile_feats, table, stage, sems):
    tile_rows, channels = tile_feats.shape
    block = stage.shape[0]
    copies = part_copies((part0, part1, part2, part3), tile_feats, sems, 0)
    for copy in copies:
        copy.start()
    table[pl.ds(tile_rows, 8), :] = jnp.zeros((8, channels), jnp.float32)
    for copy in copies:
        copy.wait()
    table[pl.ds(0, tile_rows), :] = tile_feats[...].astype(jnp.float32)

    def body(block_id, carry):
        first = pl.multiple_of(block_id * block, block)
        copy_rows(table, stage, lists, first, block)
        out[pl.ds(first, block), :] = stage[...].astype(jnp.bfloat16)
        return carry

    lax.fori_loop(0, out.shape[0] // block, body, 0)


def step_kernel(
    kernel_map, part0, part1, part2, part3, incoming, conv_hbm, down_hbm,
    grad0, grad1, grad2, grad3, link_column, link_row,
    coarse, sums,
    tile_feats, halo_feats, table, stage, gathered, pre_act, conv_weight, down_weight, tile_grad, sems,
):
    rows, channels = part0.shape
    offsets = conv_weight.shape[0]
    octants, _, out_channels = down_weight.shape
    tile_rows, halo_rows = tile_feats.shape[0], halo_feats.shape[0]
    coarse_tile = tile_grad.shape[0]
    feats = part_copies((part0, part1, part2, part3), tile_feats, sems, 0)
    halo = pltpu.make_async_copy(incoming, halo_feats, sems.at[4])
    conv = pltpu.make_async_copy(conv_hbm, conv_weight, sems.at[5])
    down = pltpu.make_async_copy(down_hbm, down_weight, sems.at[6])
    grads = part_copies((grad0, grad1, grad2, grad3), tile_grad, sems, 7)
    for copy in feats + [halo, conv, down] + grads:
        copy.start()
    pre_act[...] = jnp.zeros_like(pre_act)
    table[pl.ds(tile_rows + halo_rows, 8), :] = jnp.zeros((8, channels), jnp.float32)
    for copy in feats:
        copy.wait()
    table[pl.ds(0, tile_rows), :] = tile_feats[...].astype(jnp.float32)
    middle = offsets // 2
    own = pl.multiple_of(lax.axis_index("x") * rows, rows)
    gathered[middle] = tile_feats[pl.ds(own, rows), :]
    halo.wait()
    table[pl.ds(tile_rows, halo_rows), :] = halo_feats[...].astype(jnp.float32)
    conv.wait()

    def forward(at, previous):
        offset = at + (at >= middle).astype(jnp.int32)
        pre_act[...] += matmul(gathered[previous], conv_weight[previous])
        copy_rows(table, stage, kernel_map, offset * rows, rows)
        gathered[offset] = stage[...].astype(jnp.bfloat16)
        return offset

    last = lax.fori_loop(0, offsets - 1, forward, jnp.int32(middle))
    pre_act[...] += matmul(gathered[last], conv_weight[last])

    act = pre_act[...]
    gate = 1.0 / (1.0 + jnp.exp(-act))
    hidden_wide = act * gate
    hidden = hidden_wide.astype(jnp.bfloat16)
    hidden_turned = hidden_wide.T.astype(jnp.bfloat16)
    link = link_column[...]
    octant = link % octants
    link_turned = link_row[...]
    octant_turned = link_turned % octants
    at_parent = (link // octants) == lax.broadcasted_iota(jnp.int32, (rows, coarse_tile), 1)
    for copy in [down] + grads:
        copy.wait()
    parent_grad = matmul(at_parent.astype(jnp.bfloat16), tile_grad[...]).astype(jnp.bfloat16)
    own_term = jnp.zeros((rows, out_channels), jnp.float32)
    hidden_grad = jnp.zeros((rows, channels), jnp.float32)
    conv_rows = offsets * channels
    for o in range(octants):
        hit = octant == o
        weight = down_weight[o]
        own_term += matmul(jnp.where(hit, hidden, jnp.zeros_like(hidden)), weight)
        hidden_grad += jnp.where(hit, matmul(parent_grad, weight, 1, 1), 0.0)
        only = jnp.where(octant_turned == o, hidden_turned, jnp.zeros_like(hidden_turned))
        product = matmul(only, parent_grad).astype(jnp.bfloat16)
        sums[pl.ds(conv_rows + o * channels, channels), :] = product[:, :channels]
        sums[pl.ds(conv_rows + (octants + o) * channels, channels), :] = product[:, channels:]
    pre_grad = hidden_grad * gate * (1.0 + act * (1.0 - gate))
    pre_grad_turned = pre_grad.T.astype(jnp.bfloat16)

    from_row = (link_turned // octants) == lax.broadcasted_iota(jnp.int32, (coarse_tile, rows), 0)
    from_row = from_row.astype(jnp.bfloat16)
    high = own_term.astype(jnp.bfloat16)
    low = (own_term - high.astype(jnp.float32)).astype(jnp.bfloat16)
    coarse[...] = (matmul(from_row, high) + matmul(from_row, low)).astype(jnp.bfloat16)

    def backward(offset, carry):
        start = pl.multiple_of(offset * channels, channels)
        turned = matmul(pre_grad_turned, gathered[offset])
        sums[pl.ds(start, channels), :] = turned.T.astype(jnp.bfloat16)
        return carry

    lax.fori_loop(0, offsets, backward, 0, unroll=3)
    used = conv_rows + 2 * octants * channels
    sums[pl.ds(used, sums.shape[0] - used), :] = jnp.zeros((sums.shape[0] - used, channels), jnp.bfloat16)


def shards(features, kernel_map, send_lists, fine_to_coarse, conv_weight, down_weight, coarse_grad):
    rows, channels = features.shape
    tiles, slots = send_lists.shape[2:]
    offsets = kernel_map.shape[0]
    octants, _, out_channels = down_weight.shape
    tile_rows, halo_rows = RING_X * rows, tiles * slots
    coarse_rows = coarse_grad.shape[0]
    coarse_tile = RING_X * coarse_rows
    smem, vmem = pl.BlockSpec(memory_space=pltpu.SMEM), pl.BlockSpec(memory_space=pltpu.VMEM)
    anywhere = pl.BlockSpec(memory_space=pltpu.HBM)
    parts = share_over_x(features)
    outgoing = pl.pallas_call(
        pick_halo,
        out_shape=jax.ShapeDtypeStruct((halo_rows, channels), jnp.bfloat16),
        in_specs=[smem] + [anywhere] * 4,
        out_specs=vmem,
        scratch_shapes=[
            pltpu.VMEM((tile_rows, channels), jnp.bfloat16),
            pltpu.VMEM((tile_rows + 8, channels), jnp.float32),
            pltpu.VMEM((128, channels), jnp.float32),
            pltpu.SemaphoreType.DMA((4,)),
        ],
        compiler_params=pltpu.CompilerParams(vmem_limit_bytes=16 << 20),
        name="pick_halo",
    )(send_lists.reshape(halo_rows), *parts)
    later_grad, outgoing = lax.optimization_barrier((coarse_grad, outgoing))
    incoming = lax.all_to_all(
        outgoing.reshape(tiles, slots, channels), TILE, split_axis=0, concat_axis=0, tiled=True
    )
    grads = share_over_x(later_grad)
    x = lax.axis_index("x")
    link = lax.dynamic_slice_in_dim(fine_to_coarse, x * rows, rows)
    used = offsets * channels + 2 * octants * channels
    total = used + (-used % 512)
    coarse, sums = pl.pallas_call(
        step_kernel,
        out_shape=(
            jax.ShapeDtypeStruct((coarse_tile, out_channels), jnp.bfloat16),
            jax.ShapeDtypeStruct((total, channels), jnp.bfloat16),
        ),
        in_specs=[smem] + [anywhere] * 11 + [vmem] * 2,
        out_specs=(vmem, vmem),
        scratch_shapes=[
            pltpu.VMEM((tile_rows, channels), jnp.bfloat16),
            pltpu.VMEM((halo_rows, channels), jnp.bfloat16),
            pltpu.VMEM((tile_rows + halo_rows + 8, channels), jnp.float32),
            pltpu.VMEM((rows, channels), jnp.float32),
            pltpu.VMEM((offsets, rows, channels), jnp.bfloat16),
            pltpu.VMEM((rows, channels), jnp.float32),
            pltpu.VMEM(conv_weight.shape, jnp.bfloat16),
            pltpu.VMEM(down_weight.shape, jnp.bfloat16),
            pltpu.VMEM((coarse_tile, out_channels), jnp.bfloat16),
            pltpu.SemaphoreType.DMA((11,)),
        ],
        compiler_params=pltpu.CompilerParams(vmem_limit_bytes=56 << 20),
        name="step",
    )(
        kernel_map.reshape(offsets * rows), *parts, incoming.reshape(halo_rows, channels),
        conv_weight, down_weight, *grads, link.reshape(rows, 1), link.reshape(1, rows),
    )
    sums, coarse_out = sum_over_devices(sums, coarse)
    conv_grad = sums[: offsets * channels].reshape(offsets, channels, channels)
    down_sums = sums[offsets * channels : used]
    half = octants * channels
    down_grad = jnp.concatenate([down_sums[:half], down_sums[half:]], axis=1)
    down_grad = down_grad.reshape(octants, channels, out_channels)
    return (coarse_out, conv_grad, down_grad)


def solution(mesh):
    fine_mesh = Mesh(mesh.devices.reshape(RING_Y, DEPTH_Z, CORES, RING_X), AXES)
    placed = (
        P(AXES, None),
        P(None, AXES),
        P(TILE, "x", None, None),
        P(TILE),
        P(),
        P(),
        P(AXES, None),
    )
    return jax.shard_map(
        shards,
        mesh=fine_mesh,
        in_specs=placed,
        out_specs=(P(AXES, None), P(), P()),
        check_vma=False,
    )
```

```python
import jax
import jax.numpy as jnp
from jax import lax
from jax.experimental import pallas as pl
from jax.experimental.pallas import tpu as pltpu
from jax.sharding import Mesh, PartitionSpec as P

RING_Y, DEPTH_Z, CORES, RING_X = 4, 8, 2, 4
AXES = ("y", "z", "core", "x")
TILE = ("y", "z", "core")
UNROLL = 32


def device_index(place):
    tile = (place[0] * DEPTH_Z + place[1]) * CORES + place[2]
    return tile * RING_X + place[3]


def partner_pairs(partner):
    pairs = []
    for y in range(RING_Y):
        for z in range(DEPTH_Z):
            for core in range(CORES):
                for x in range(RING_X):
                    place = (y, z, core, x)
                    pairs.append((device_index(place), device_index(partner(*place))))
    return pairs


def send(value, partner):
    return lax.ppermute(value, AXES, partner_pairs(partner))


def across_core(y, z, core, x):
    return (y, z, 1 - core, x)


def square(step, hop):
    def partner(y, z, core, x):
        return (y ^ (hop if step & 2 else 0), z, core, x ^ (hop if step & 1 else 0))

    return partner


def first_ring(step):
    return lambda y, z, core, x: square(step, 1 if core else 3)(y, z, core, x)


def second_ring(step):
    return lambda y, z, core, x: square(step, 3 if core else 1)(y, z, core, x)


def along_z(step):
    return lambda y, z, core, x: (y, z ^ step, core, x)


def narrow(value):
    return value.astype(jnp.bfloat16)


def wide(value):
    return value.astype(jnp.float32)


def pick(parts, digit):
    return lax.dynamic_index_in_dim(parts, digit, 0, keepdims=False)


def scatter_pair(parts, digit, partner):
    other = send(pick(parts, 1 - digit), partner)
    return narrow(wide(pick(parts, digit)) + wide(other))


def scatter_ring(parts, digit, ring):
    received = [send(pick(parts, digit ^ step), ring(step)) for step in (1, 2, 3)]
    total = wide(pick(parts, digit))
    for part in received:
        total = total + wide(part)
    return narrow(total)


def swap(first, second, flip):
    return jnp.where(flip, second, first), jnp.where(flip, first, second)


def gather_pair(part, digit, partner):
    other = send(part, partner)
    return jnp.stack(swap(part, other, digit == 1))


def gather_ring(part, digit, ring):
    parts = [part] + [send(part, ring(step)) for step in (1, 2, 3)]
    low, high = digit % 2 == 1, digit // 2 == 1
    first, second = swap(parts[0], parts[1], low)
    third, fourth = swap(parts[2], parts[3], low)
    first, third = swap(first, third, high)
    second, fourth = swap(second, fourth, high)
    return jnp.stack([first, second, third, fourth])


def sum_over_devices(partial_sums, coarse):
    y, z, core, x = (lax.axis_index(name) for name in AXES)
    near_x, near_y = (x ^ (x >> 1)) & 1, (y ^ (y >> 1)) & 1
    far_x, far_y = x >> 1, y >> 1
    near, far = near_x + 2 * near_y, far_x + 2 * far_y
    ring_one = jnp.where(core == 0, far, near)
    ring_two = jnp.where(core == 0, near, far)
    rows = partial_sums.shape[0] // (CORES * RING_X * RING_Y)
    lanes = partial_sums.shape[1]
    parts = partial_sums.reshape(CORES, RING_X * RING_Y * rows, lanes)
    part = scatter_pair(parts, core, across_core)
    part = scatter_ring(part.reshape(RING_X, RING_Y * rows, lanes), ring_one, first_ring)
    part, coarse = lax.optimization_barrier((part, coarse))
    shares = coarse.reshape(RING_X, coarse.shape[0] // RING_X, coarse.shape[1])
    shares = lax.all_to_all(shares, "x", split_axis=0, concat_axis=0, tiled=True)
    coarse_out = narrow(jnp.sum(wide(shares), axis=0))
    part = scatter_ring(part.reshape(RING_Y, rows, lanes), ring_two, second_ring)
    for step in (1, 2, 7):
        part = narrow(wide(part) + wide(send(part, along_z(step))))
    part, coarse_out = lax.optimization_barrier((part, coarse_out))
    part = gather_ring(part, ring_two, second_ring).reshape(RING_Y * rows, lanes)
    part = gather_ring(part, ring_one, first_ring).reshape(RING_X * RING_Y * rows, lanes)
    return wide(gather_pair(part, core, across_core)).reshape(partial_sums.shape), coarse_out


def ring_x(step):
    return lambda y, z, core, x: (y, z, core, x ^ step)


def share_over_x(value):
    return [value] + [send(value, ring_x(step)) for step in (1, 2, 3)]


def part_copies(parts, target, sems, first):
    x = lax.axis_index("x")
    rows = parts[0].shape[0]
    copies = []
    for step, part in enumerate(parts):
        place = target.at[pl.ds(pl.multiple_of((x ^ step) * rows, rows), rows)]
        copies.append(pltpu.make_async_copy(part, place, sems.at[first + step]))
    return copies


def copy_rows(table, target, picks, first, count):
    for start in range(0, count, UNROLL):
        places = range(start, min(start + UNROLL, count))
        rows = [table[pl.ds(picks[first + at], 1), :] for at in places]
        for at, row in zip(places, rows):
            target[at : at + 1, :] = row


def matmul(left, right, left_dim=1, right_dim=0):
    return lax.dot_general(
        left, right, (((left_dim,), (right_dim,)), ((), ())), preferred_element_type=jnp.float32
    )


def pick_halo(lists, part0, part1, part2, part3, out, tile_feats, table, stage, sems):
    tile_rows, channels = tile_feats.shape
    block = stage.shape[0]
    copies = part_copies((part0, part1, part2, part3), tile_feats, sems, 0)
    for copy in copies:
        copy.start()
    table[pl.ds(tile_rows, 8), :] = jnp.zeros((8, channels), jnp.float32)
    for copy in copies:
        copy.wait()
    table[pl.ds(0, tile_rows), :] = tile_feats[...].astype(jnp.float32)

    def body(block_id, carry):
        first = pl.multiple_of(block_id * block, block)
        copy_rows(table, stage, lists, first, block)
        out[pl.ds(first, block), :] = stage[...].astype(jnp.bfloat16)
        return carry

    lax.fori_loop(0, out.shape[0] // block, body, 0)


def step_kernel(
    kernel_map, part0, part1, part2, part3, incoming, conv_hbm, down_hbm,
    grad0, grad1, grad2, grad3, link_column, link_row,
    coarse, sums,
    tile_feats, table, stage, gathered, pre_act, conv_weight, down_weight, tile_grad, sems,
):
    rows, channels = part0.shape
    offsets = conv_weight.shape[0]
    octants, _, out_channels = down_weight.shape
    tile_rows, halo_rows = tile_feats.shape[0], incoming.shape[0]
    coarse_tile = tile_grad.shape[0]
    feats = part_copies((part0, part1, part2, part3), tile_feats, sems, 0)
    conv = pltpu.make_async_copy(conv_hbm, conv_weight, sems.at[4])
    down = pltpu.make_async_copy(down_hbm, down_weight, sems.at[5])
    grads = part_copies((grad0, grad1, grad2, grad3), tile_grad, sems, 6)
    for copy in feats + [conv, down] + grads:
        copy.start()
    pre_act[...] = jnp.zeros_like(pre_act)
    table[pl.ds(tile_rows + halo_rows, 8), :] = jnp.zeros((8, channels), jnp.float32)
    for copy in feats:
        copy.wait()
    table[pl.ds(0, tile_rows), :] = tile_feats[...].astype(jnp.float32)
    middle = offsets // 2
    own = pl.multiple_of(lax.axis_index("x") * rows, rows)
    gathered[middle] = tile_feats[pl.ds(own, rows), :]
    table[pl.ds(tile_rows, halo_rows), :] = incoming[...].astype(jnp.float32)
    conv.wait()

    def forward(at, previous):
        offset = at + (at >= middle).astype(jnp.int32)
        pre_act[...] += matmul(gathered[previous], conv_weight[previous])
        copy_rows(table, stage, kernel_map, offset * rows, rows)
        gathered[offset] = stage[...].astype(jnp.bfloat16)
        return offset

    last = lax.fori_loop(0, offsets - 1, forward, jnp.int32(middle))
    pre_act[...] += matmul(gathered[last], conv_weight[last])

    act = pre_act[...]
    gate = 1.0 / (1.0 + jnp.exp(-act))
    hidden_wide = act * gate
    hidden = hidden_wide.astype(jnp.bfloat16)
    hidden_turned = hidden_wide.T.astype(jnp.bfloat16)
    link = link_column[...]
    octant = link % octants
    link_turned = link_row[...]
    octant_turned = link_turned % octants
    at_parent = (link // octants) == lax.broadcasted_iota(jnp.int32, (rows, coarse_tile), 1)
    for copy in [down] + grads:
        copy.wait()
    parent_grad = matmul(at_parent.astype(jnp.bfloat16), tile_grad[...]).astype(jnp.bfloat16)
    own_term = jnp.zeros((rows, out_channels), jnp.float32)
    hidden_grad = jnp.zeros((rows, channels), jnp.float32)
    conv_rows = offsets * channels
    for o in range(octants):
        hit = octant == o
        weight = down_weight[o]
        own_term += matmul(jnp.where(hit, hidden, jnp.zeros_like(hidden)), weight)
        hidden_grad += jnp.where(hit, matmul(parent_grad, weight, 1, 1), 0.0)
        only = jnp.where(octant_turned == o, hidden_turned, jnp.zeros_like(hidden_turned))
        product = matmul(only, parent_grad).astype(jnp.bfloat16)
        sums[pl.ds(conv_rows + o * channels, channels), :] = product[:, :channels]
        sums[pl.ds(conv_rows + (octants + o) * channels, channels), :] = product[:, channels:]
    pre_grad = hidden_grad * gate * (1.0 + act * (1.0 - gate))
    pre_grad_turned = pre_grad.T.astype(jnp.bfloat16)

    from_row = (link_turned // octants) == lax.broadcasted_iota(jnp.int32, (coarse_tile, rows), 0)
    from_row = from_row.astype(jnp.bfloat16)
    high = own_term.astype(jnp.bfloat16)
    low = (own_term - high.astype(jnp.float32)).astype(jnp.bfloat16)
    coarse[...] = (matmul(from_row, high) + matmul(from_row, low)).astype(jnp.bfloat16)

    def backward(offset, carry):
        start = pl.multiple_of(offset * channels, channels)
        turned = matmul(pre_grad_turned, gathered[offset])
        sums[pl.ds(start, channels), :] = turned.T.astype(jnp.bfloat16)
        return carry

    lax.fori_loop(0, offsets, backward, 0, unroll=3)
    used = conv_rows + 2 * octants * channels
    sums[pl.ds(used, sums.shape[0] - used), :] = jnp.zeros((sums.shape[0] - used, channels), jnp.bfloat16)


def shards(features, kernel_map, send_lists, fine_to_coarse, conv_weight, down_weight, coarse_grad):
    rows, channels = features.shape
    tiles, slots = send_lists.shape[2:]
    offsets = kernel_map.shape[0]
    octants, _, out_channels = down_weight.shape
    tile_rows, halo_rows = RING_X * rows, tiles * slots
    coarse_rows = coarse_grad.shape[0]
    coarse_tile = RING_X * coarse_rows
    smem, vmem = pl.BlockSpec(memory_space=pltpu.SMEM), pl.BlockSpec(memory_space=pltpu.VMEM)
    anywhere = pl.BlockSpec(memory_space=pltpu.HBM)
    parts = share_over_x(features)
    outgoing = pl.pallas_call(
        pick_halo,
        out_shape=jax.ShapeDtypeStruct((halo_rows, channels), jnp.bfloat16),
        in_specs=[smem] + [anywhere] * 4,
        out_specs=vmem,
        scratch_shapes=[
            pltpu.VMEM((tile_rows, channels), jnp.bfloat16),
            pltpu.VMEM((tile_rows + 8, channels), jnp.float32),
            pltpu.VMEM((128, channels), jnp.float32),
            pltpu.SemaphoreType.DMA((4,)),
        ],
        compiler_params=pltpu.CompilerParams(vmem_limit_bytes=56 << 20),
        name="pick_halo",
    )(send_lists.reshape(halo_rows), *parts)
    later_grad, outgoing = lax.optimization_barrier((coarse_grad, outgoing))
    incoming = lax.all_to_all(
        outgoing.reshape(tiles, slots, channels), TILE, split_axis=0, concat_axis=0, tiled=True
    )
    grads = share_over_x(later_grad)
    x = lax.axis_index("x")
    link = lax.dynamic_slice_in_dim(fine_to_coarse, x * rows, rows)
    used = offsets * channels + 2 * octants * channels
    total = used + (-used % 512)
    coarse, sums = pl.pallas_call(
        step_kernel,
        out_shape=(
            jax.ShapeDtypeStruct((coarse_tile, out_channels), jnp.bfloat16),
            jax.ShapeDtypeStruct((total, channels), jnp.bfloat16),
        ),
        in_specs=[smem] + [anywhere] * 4 + [vmem] + [anywhere] * 6 + [vmem] * 2,
        out_specs=(vmem, vmem),
        scratch_shapes=[
            pltpu.VMEM((tile_rows, channels), jnp.bfloat16),
            pltpu.VMEM((tile_rows + halo_rows + 8, channels), jnp.float32),
            pltpu.VMEM((rows, channels), jnp.float32),
            pltpu.VMEM((offsets, rows, channels), jnp.bfloat16),
            pltpu.VMEM((rows, channels), jnp.float32),
            pltpu.VMEM(conv_weight.shape, jnp.bfloat16),
            pltpu.VMEM(down_weight.shape, jnp.bfloat16),
            pltpu.VMEM((coarse_tile, out_channels), jnp.bfloat16),
            pltpu.SemaphoreType.DMA((10,)),
        ],
        compiler_params=pltpu.CompilerParams(vmem_limit_bytes=56 << 20),
        name="step",
    )(
        kernel_map.reshape(offsets * rows), *parts, incoming.reshape(halo_rows, channels),
        conv_weight, down_weight, *grads, link.reshape(rows, 1), link.reshape(1, rows),
    )
    sums, coarse_out = sum_over_devices(sums, coarse)
    conv_grad = sums[: offsets * channels].reshape(offsets, channels, channels)
    down_sums = sums[offsets * channels : used]
    half = octants * channels
    down_grad = jnp.concatenate([down_sums[:half], down_sums[half:]], axis=1)
    down_grad = down_grad.reshape(octants, channels, out_channels)
    return (coarse_out, conv_grad, down_grad)


def solution(mesh):
    fine_mesh = Mesh(mesh.devices.reshape(RING_Y, DEPTH_Z, CORES, RING_X), AXES)
    placed = (
        P(AXES, None),
        P(None, AXES),
        P(TILE, "x", None, None),
        P(TILE),
        P(),
        P(),
        P(AXES, None),
    )
    return jax.shard_map(
        shards,
        mesh=fine_mesh,
        in_specs=placed,
        out_specs=(P(AXES, None), P(), P()),
        check_vma=False,
    )
```

```python
import jax
import jax.numpy as jnp
from jax import lax
from jax.experimental import pallas as pl
from jax.experimental.pallas import tpu as pltpu
from jax.sharding import Mesh, PartitionSpec as P

RING_Y, DEPTH_Z, CORES, RING_X = 4, 8, 2, 4
AXES = ("y", "z", "core", "x")
TILE = ("y", "z", "core")
UNROLL = 32
GRID_W, GRID_H = 8, 4


def device_index(place):
    tile = (place[0] * DEPTH_Z + place[1]) * CORES + place[2]
    return tile * RING_X + place[3]


def partner_pairs(partner):
    pairs = []
    for y in range(RING_Y):
        for z in range(DEPTH_Z):
            for core in range(CORES):
                for x in range(RING_X):
                    place = (y, z, core, x)
                    pairs.append((device_index(place), device_index(partner(*place))))
    return pairs


def send(value, partner):
    return lax.ppermute(value, AXES, partner_pairs(partner))


def across_core(y, z, core, x):
    return (y, z, 1 - core, x)


def square(step, hop):
    def partner(y, z, core, x):
        return (y ^ (hop if step & 2 else 0), z, core, x ^ (hop if step & 1 else 0))

    return partner


def first_ring(step):
    return lambda y, z, core, x: square(step, 1 if core else 3)(y, z, core, x)


def second_ring(step):
    return lambda y, z, core, x: square(step, 3 if core else 1)(y, z, core, x)


def along_z(step):
    return lambda y, z, core, x: (y, z ^ step, core, x)


def narrow(value):
    return value.astype(jnp.bfloat16)


def wide(value):
    return value.astype(jnp.float32)


def pick(parts, digit):
    return lax.dynamic_index_in_dim(parts, digit, 0, keepdims=False)


def scatter_ring(parts, digit, ring):
    received = [send(pick(parts, digit ^ step), ring(step)) for step in (1, 2, 3)]
    total = wide(pick(parts, digit))
    for part in received:
        total = total + wide(part)
    return narrow(total)


def swap(first, second, flip):
    return jnp.where(flip, second, first), jnp.where(flip, first, second)


def gather_pair(part, digit, partner):
    other = send(part, partner)
    return jnp.stack(swap(part, other, digit == 1))


def gather_ring(part, digit, ring):
    parts = [part] + [send(part, ring(step)) for step in (1, 2, 3)]
    low, high = digit % 2 == 1, digit // 2 == 1
    first, second = swap(parts[0], parts[1], low)
    third, fourth = swap(parts[2], parts[3], low)
    first, third = swap(first, third, high)
    second, fourth = swap(second, fourth, high)
    return jnp.stack([first, second, third, fourth])


def sum_over_devices(mine, other, coarse):
    y, z, core, x = (lax.axis_index(name) for name in AXES)
    near_x, near_y = (x ^ (x >> 1)) & 1, (y ^ (y >> 1)) & 1
    far_x, far_y = x >> 1, y >> 1
    near, far = near_x + 2 * near_y, far_x + 2 * far_y
    ring_one = jnp.where(core == 0, far, near)
    ring_two = jnp.where(core == 0, near, far)
    rows, lanes = mine.shape[0] // (RING_X * RING_Y), mine.shape[1]
    part = narrow(wide(mine) + wide(send(other, across_core)))
    part = scatter_ring(part.reshape(RING_X, RING_Y * rows, lanes), ring_one, first_ring)
    part, coarse = lax.optimization_barrier((part, coarse))
    shares = coarse.reshape(RING_X, coarse.shape[0] // RING_X, coarse.shape[1])
    shares = lax.all_to_all(shares, "x", split_axis=0, concat_axis=0, tiled=True)
    coarse_out = narrow(jnp.sum(wide(shares), axis=0))
    part = scatter_ring(part.reshape(RING_Y, rows, lanes), ring_two, second_ring)
    for step in (1, 2, 7):
        part = narrow(wide(part) + wide(send(part, along_z(step))))
    part, coarse_out = lax.optimization_barrier((part, coarse_out))
    part = gather_ring(part, ring_two, second_ring).reshape(RING_Y * rows, lanes)
    part = gather_ring(part, ring_one, first_ring).reshape(RING_X * RING_Y * rows, lanes)
    return wide(gather_pair(part, core, across_core)).reshape(-1, lanes), coarse_out


def ring_x(step):
    return lambda y, z, core, x: (y, z, core, x ^ step)


def share_over_x(value):
    return [value] + [send(value, ring_x(step)) for step in (1, 2, 3)]


def part_copies(parts, target, sems, first):
    x = lax.axis_index("x")
    rows = parts[0].shape[0]
    copies = []
    for step, part in enumerate(parts):
        place = target.at[pl.ds(pl.multiple_of((x ^ step) * rows, rows), rows)]
        copies.append(pltpu.make_async_copy(part, place, sems.at[first + step]))
    return copies


def copy_rows(table, target, picks, first, count):
    for start in range(0, count, UNROLL):
        places = range(start, min(start + UNROLL, count))
        rows = [table[pl.ds(picks[first + at], 1), :] for at in places]
        for at, row in zip(places, rows):
            target[at : at + 1, :] = row


def matmul(left, right, left_dim=1, right_dim=0):
    return lax.dot_general(
        left, right, (((left_dim,), (right_dim,)), ((), ())), preferred_element_type=jnp.float32
    )


def pick_halo(lists, part0, part1, part2, part3, out, tile_feats, table, stage, sems):
    tile_rows, channels = tile_feats.shape
    slots = stage.shape[0]
    copies = part_copies((part0, part1, part2, part3), tile_feats, sems, 0)
    for copy in copies:
        copy.start()
    table[pl.ds(tile_rows, 8), :] = jnp.zeros((8, channels), jnp.float32)
    out[...] = jnp.zeros_like(out)
    y, z, core = (lax.axis_index(name) for name in TILE)
    own = (y * DEPTH_Z + z) * CORES + core
    for copy in copies:
        copy.wait()
    table[pl.ds(0, tile_rows), :] = tile_feats[...].astype(jnp.float32)
    planes, lines = RING_X * RING_Y * DEPTH_Z * CORES // (RING_X * GRID_W * GRID_H), GRID_H

    def body(at, carry):
        line = own % (GRID_W * GRID_H) // GRID_W + at // 3 % 3 - 1
        column = own % GRID_W + at % 3 - 1
        inside = (line >= 0) & (line < lines) & (column >= 0) & (column < GRID_W)
        tile = (at // 9 % planes * GRID_H + line) * GRID_W + column
        tile = jnp.where(inside, tile, own)
        first = pl.multiple_of(tile * slots, slots)
        copy_rows(table, stage, lists, first, slots)
        out[pl.ds(first, slots), :] = stage[...].astype(jnp.bfloat16)
        return carry

    lax.fori_loop(0, 9 * planes, body, 0)


def grad_kernel(
    grad0, grad1, grad2, grad3, down_weight, link_column, parent_out, hidden_out, tile_grad, sems
):
    copies = part_copies((grad0, grad1, grad2, grad3), tile_grad, sems, 0)
    for copy in copies:
        copy.start()
    octants = down_weight.shape[0]
    rows, channels = hidden_out.shape
    link = link_column[...]
    octant = link % octants
    columns = lax.broadcasted_iota(jnp.int32, (rows, tile_grad.shape[0]), 1)
    at_parent = ((link // octants) == columns).astype(jnp.bfloat16)
    for copy in copies:
        copy.wait()
    parent_grad = matmul(at_parent, tile_grad[...]).astype(jnp.bfloat16)
    hidden_grad = jnp.zeros((rows, channels), jnp.float32)
    for o in range(octants):
        back = matmul(parent_grad, down_weight[o], 1, 1)
        hidden_grad += jnp.where(octant == o, back, 0.0)
    parent_out[...] = parent_grad
    hidden_out[...] = hidden_grad


def step_kernel(
    kernel_map, part0, part1, part2, part3, incoming, conv_hbm, down_hbm, parent_hbm, back_hbm,
    link_column, link_row,
    coarse, mine, other,
    tile_feats, table, stage, gathered, pre_act, conv_weight, down_weight, parent_grad, back_grad, sems,
):
    rows, channels = part0.shape
    offsets = conv_weight.shape[0]
    octants, _, out_channels = down_weight.shape
    tile_rows, halo_rows = tile_feats.shape[0], incoming.shape[0]
    coarse_tile = coarse.shape[0]
    feats = part_copies((part0, part1, part2, part3), tile_feats, sems, 0)
    conv = pltpu.make_async_copy(conv_hbm, conv_weight, sems.at[4])
    late = [
        pltpu.make_async_copy(down_hbm, down_weight, sems.at[5]),
        pltpu.make_async_copy(parent_hbm, parent_grad, sems.at[6]),
        pltpu.make_async_copy(back_hbm, back_grad, sems.at[7]),
    ]
    for copy in feats + [conv] + late:
        copy.start()
    pre_act[...] = jnp.zeros_like(pre_act)
    table[pl.ds(tile_rows + halo_rows, 8), :] = jnp.zeros((8, channels), jnp.float32)
    table[pl.ds(tile_rows, halo_rows), :] = incoming[...].astype(jnp.float32)
    for copy in feats:
        copy.wait()
    table[pl.ds(0, tile_rows), :] = tile_feats[...].astype(jnp.float32)
    middle = offsets // 2
    own = pl.multiple_of(lax.axis_index("x") * rows, rows)
    gathered[middle] = tile_feats[pl.ds(own, rows), :]
    conv.wait()

    def forward(at, previous):
        offset = at + (at >= middle).astype(jnp.int32)
        pre_act[...] += matmul(gathered[previous], conv_weight[previous])
        copy_rows(table, stage, kernel_map, offset * rows, rows)
        gathered[offset] = stage[...].astype(jnp.bfloat16)
        return offset

    last = lax.fori_loop(0, offsets - 1, forward, jnp.int32(middle))
    for copy in late:
        copy.wait()
    act = pre_act[...] + matmul(gathered[last], conv_weight[last])
    gate = 1.0 / (1.0 + jnp.exp(-act))
    hidden_wide = act * gate
    hidden = hidden_wide.astype(jnp.bfloat16)
    hidden_turned = hidden_wide.T.astype(jnp.bfloat16)
    pre_grad = back_grad[...] * gate * (1.0 + act * (1.0 - gate))
    pre_grad_turned = pre_grad.T.astype(jnp.bfloat16)
    octant = link_column[...] % octants
    link_turned = link_row[...]
    octant_turned = link_turned % octants
    own_term = jnp.zeros((rows, out_channels), jnp.float32)
    for o in range(octants):
        only = jnp.where(octant == o, hidden, jnp.zeros_like(hidden))
        own_term += matmul(only, down_weight[o])
    from_row = (link_turned // octants) == lax.broadcasted_iota(jnp.int32, (coarse_tile, rows), 0)
    from_row = from_row.astype(jnp.bfloat16)
    high = own_term.astype(jnp.bfloat16)
    low = (own_term - high.astype(jnp.float32)).astype(jnp.bfloat16)
    coarse[...] = (matmul(from_row, high) + matmul(from_row, low)).astype(jnp.bfloat16)

    half_blocks = mine.shape[0] // channels
    down_first = offsets - half_blocks

    def fill(first, second):
        def backward(target, start):
            def body(at, carry):
                turned = matmul(pre_grad_turned, gathered[start + at])
                place = pl.ds(pl.multiple_of(at * channels, channels), channels)
                target[place, :] = turned.T.astype(jnp.bfloat16)
                return carry

            return body

        lax.fori_loop(0, half_blocks, backward(first, 0), 0, unroll=2)
        lax.fori_loop(0, down_first, backward(second, half_blocks), 0, unroll=True)
        for o in range(octants):
            only = jnp.where(octant_turned == o, hidden_turned, jnp.zeros_like(hidden_turned))
            product = matmul(only, parent_grad[...]).astype(jnp.bfloat16)
            left, right = (down_first + o) * channels, (down_first + octants + o) * channels
            second[pl.ds(left, channels), :] = product[:, :channels]
            second[pl.ds(right, channels), :] = product[:, channels:]
        used = (down_first + 2 * octants) * channels
        second[pl.ds(used, second.shape[0] - used), :] = jnp.zeros(
            (second.shape[0] - used, channels), jnp.bfloat16
        )

    core = lax.axis_index("core")

    @pl.when(core == 0)
    def _():
        fill(mine, other)

    @pl.when(core == 1)
    def _():
        fill(other, mine)


def shards(features, kernel_map, send_lists, fine_to_coarse, conv_weight, down_weight, coarse_grad):
    rows, channels = features.shape
    tiles, slots = send_lists.shape[2:]
    offsets = kernel_map.shape[0]
    octants, _, out_channels = down_weight.shape
    tile_rows, halo_rows = RING_X * rows, tiles * slots
    coarse_rows = coarse_grad.shape[0]
    coarse_tile = RING_X * coarse_rows
    smem, vmem = pl.BlockSpec(memory_space=pltpu.SMEM), pl.BlockSpec(memory_space=pltpu.VMEM)
    anywhere = pl.BlockSpec(memory_space=pltpu.HBM)
    parts = share_over_x(features)
    outgoing = pl.pallas_call(
        pick_halo,
        out_shape=jax.ShapeDtypeStruct((halo_rows, channels), jnp.bfloat16),
        in_specs=[smem] + [anywhere] * 4,
        out_specs=vmem,
        scratch_shapes=[
            pltpu.VMEM((tile_rows, channels), jnp.bfloat16),
            pltpu.VMEM((tile_rows + 8, channels), jnp.float32),
            pltpu.VMEM((slots, channels), jnp.float32),
            pltpu.SemaphoreType.DMA((4,)),
        ],
        compiler_params=pltpu.CompilerParams(vmem_limit_bytes=56 << 20),
        name="pick_halo",
    )(send_lists.reshape(halo_rows), *parts)
    later_grad, outgoing = lax.optimization_barrier((coarse_grad, outgoing))
    incoming = lax.all_to_all(
        outgoing.reshape(tiles, slots, channels), TILE, split_axis=0, concat_axis=0, tiled=True
    )
    grads = share_over_x(later_grad)
    x = lax.axis_index("x")
    link = lax.dynamic_slice_in_dim(fine_to_coarse, x * rows, rows)
    used = offsets * channels + 2 * octants * channels
    total = used + (-used % 512)
    link_column, link_row = link.reshape(rows, 1), link.reshape(1, rows)
    parent_grad, back_grad = pl.pallas_call(
        grad_kernel,
        out_shape=(
            jax.ShapeDtypeStruct((rows, out_channels), jnp.bfloat16),
            jax.ShapeDtypeStruct((rows, channels), jnp.float32),
        ),
        in_specs=[anywhere] * 4 + [vmem] * 2,
        out_specs=(vmem, vmem),
        scratch_shapes=[
            pltpu.VMEM((coarse_tile, out_channels), jnp.bfloat16),
            pltpu.SemaphoreType.DMA((4,)),
        ],
        compiler_params=pltpu.CompilerParams(vmem_limit_bytes=56 << 20),
        name="coarse_back",
    )(*grads, down_weight, link_column)
    half = total // CORES
    coarse, mine, other = pl.pallas_call(
        step_kernel,
        out_shape=(
            jax.ShapeDtypeStruct((coarse_tile, out_channels), jnp.bfloat16),
            jax.ShapeDtypeStruct((half, channels), jnp.bfloat16),
            jax.ShapeDtypeStruct((half, channels), jnp.bfloat16),
        ),
        in_specs=[smem] + [anywhere] * 4 + [vmem] + [anywhere] * 4 + [vmem] * 2,
        out_specs=(vmem, vmem, vmem),
        scratch_shapes=[
            pltpu.VMEM((tile_rows, channels), jnp.bfloat16),
            pltpu.VMEM((tile_rows + halo_rows + 8, channels), jnp.float32),
            pltpu.VMEM((rows, channels), jnp.float32),
            pltpu.VMEM((offsets, rows, channels), jnp.bfloat16),
            pltpu.VMEM((rows, channels), jnp.float32),
            pltpu.VMEM(conv_weight.shape, jnp.bfloat16),
            pltpu.VMEM(down_weight.shape, jnp.bfloat16),
            pltpu.VMEM((rows, out_channels), jnp.bfloat16),
            pltpu.VMEM((rows, channels), jnp.float32),
            pltpu.SemaphoreType.DMA((8,)),
        ],
        compiler_params=pltpu.CompilerParams(vmem_limit_bytes=56 << 20),
        name="step",
    )(
        kernel_map.reshape(offsets * rows), *parts, incoming.reshape(halo_rows, channels),
        conv_weight, down_weight, parent_grad, back_grad, link_column, link_row,
    )
    sums, coarse_out = sum_over_devices(mine, other, coarse)
    conv_grad = sums[: offsets * channels].reshape(offsets, channels, channels)
    down_sums = sums[offsets * channels : used]
    half = octants * channels
    down_grad = jnp.concatenate([down_sums[:half], down_sums[half:]], axis=1)
    down_grad = down_grad.reshape(octants, channels, out_channels)
    return (coarse_out, conv_grad, down_grad)


def solution(mesh):
    fine_mesh = Mesh(mesh.devices.reshape(RING_Y, DEPTH_Z, CORES, RING_X), AXES)
    placed = (
        P(AXES, None),
        P(None, AXES),
        P(TILE, "x", None, None),
        P(TILE),
        P(),
        P(),
        P(AXES, None),
    )
    return jax.shard_map(
        shards,
        mesh=fine_mesh,
        in_specs=placed,
        out_specs=(P(AXES, None), P(), P()),
        check_vma=False,
    )
```

```python
import jax
import jax.numpy as jnp
from jax import lax
from jax.experimental import pallas as pl
from jax.experimental.pallas import tpu as pltpu
from jax.sharding import Mesh, PartitionSpec as P

RING_Y, DEPTH_Z, CORES, RING_X = 4, 8, 2, 4
AXES = ("y", "z", "core", "x")
TILE = ("y", "z", "core")
UNROLL = 32
GRID_W, GRID_H = 8, 4


def device_index(place):
    tile = (place[0] * DEPTH_Z + place[1]) * CORES + place[2]
    return tile * RING_X + place[3]


def partner_pairs(partner):
    pairs = []
    for y in range(RING_Y):
        for z in range(DEPTH_Z):
            for core in range(CORES):
                for x in range(RING_X):
                    place = (y, z, core, x)
                    pairs.append((device_index(place), device_index(partner(*place))))
    return pairs


def send(value, partner):
    return lax.ppermute(value, AXES, partner_pairs(partner))


def across_core(y, z, core, x):
    return (y, z, 1 - core, x)


def square(step, hop):
    def partner(y, z, core, x):
        return (y ^ (hop if step & 2 else 0), z, core, x ^ (hop if step & 1 else 0))

    return partner


def ring_digits(y, z, core, x):
    near = ((x ^ (x >> 1)) & 1) + 2 * ((y ^ (y >> 1)) & 1)
    far = (x >> 1) + 2 * (y >> 1)
    return (far, near) if core == 0 else (near, far)


def square_groups():
    groups = {}
    for y in range(RING_Y):
        for z in range(DEPTH_Z):
            for core in range(CORES):
                for x in range(RING_X):
                    digit, rest = ring_digits(y, z, core, x)
                    members = groups.setdefault((z, core, rest), [0] * 4)
                    members[digit] = device_index((y, z, core, x))
    return [groups[key] for key in sorted(groups)]


def exchange_first(parts):
    return lax.all_to_all(
        parts, AXES, split_axis=0, concat_axis=0, tiled=True, axis_index_groups=square_groups()
    )


def second_ring(step):
    return lambda y, z, core, x: square(step, 3 if core else 1)(y, z, core, x)


def along_z(step):
    return lambda y, z, core, x: (y, z ^ step, core, x)


def narrow(value):
    return value.astype(jnp.bfloat16)


def wide(value):
    return value.astype(jnp.float32)


def pick(parts, digit):
    return lax.dynamic_index_in_dim(parts, digit, 0, keepdims=False)


def scatter_ring(parts, digit, ring):
    received = [send(pick(parts, digit ^ step), ring(step)) for step in (1, 2, 3)]
    total = wide(pick(parts, digit))
    for part in received:
        total = total + wide(part)
    return narrow(total)


def swap(first, second, flip):
    return jnp.where(flip, second, first), jnp.where(flip, first, second)


def gather_pair(part, digit, partner):
    other = send(part, partner)
    return jnp.stack(swap(part, other, digit == 1))


def gather_ring(part, digit, ring):
    parts = [part] + [send(part, ring(step)) for step in (1, 2, 3)]
    low, high = digit % 2 == 1, digit // 2 == 1
    first, second = swap(parts[0], parts[1], low)
    third, fourth = swap(parts[2], parts[3], low)
    first, third = swap(first, third, high)
    second, fourth = swap(second, fourth, high)
    return jnp.stack([first, second, third, fourth])


def sum_over_devices(mine, other, coarse):
    y, z, core, x = (lax.axis_index(name) for name in AXES)
    near = ((x ^ (x >> 1)) & 1) + 2 * ((y ^ (y >> 1)) & 1)
    far = (x >> 1) + 2 * (y >> 1)
    ring_two = jnp.where(core == 0, near, far)
    rows, lanes = mine.shape[0] // (RING_X * RING_Y), mine.shape[1]
    part = narrow(wide(mine) + wide(send(other, across_core)))
    parts = exchange_first(part.reshape(4, 4 * rows, lanes))
    part = narrow(jnp.sum(wide(parts), axis=0))
    shares = coarse.reshape(RING_X, coarse.shape[0] // RING_X, coarse.shape[1])
    shares = lax.all_to_all(shares, "x", split_axis=0, concat_axis=0, tiled=True)
    part = scatter_ring(part.reshape(4, rows, lanes), ring_two, second_ring)
    for step in (1, 2, 7):
        part = narrow(wide(part) + wide(send(part, along_z(step))))
    part, shares = lax.optimization_barrier((part, shares))
    part = gather_ring(part, ring_two, second_ring).reshape(4 * rows, lanes)
    spread, shares = lax.optimization_barrier(
        (jnp.broadcast_to(part[None], (4, 4 * rows, lanes)), shares)
    )
    part = exchange_first(spread).reshape(16 * rows, lanes)
    coarse_out = narrow(jnp.sum(wide(shares), axis=0))
    part, coarse_out = lax.optimization_barrier((part, coarse_out))
    return wide(gather_pair(part, core, across_core)).reshape(-1, lanes), coarse_out


def ring_x(step):
    return lambda y, z, core, x: (y, z, core, x ^ step)


def share_over_x(value):
    return [value] + [send(value, ring_x(step)) for step in (1, 2, 3)]


def part_copies(parts, target, sems, first):
    x = lax.axis_index("x")
    rows = parts[0].shape[0]
    copies = []
    for step, part in enumerate(parts):
        place = target.at[pl.ds(pl.multiple_of((x ^ step) * rows, rows), rows)]
        copies.append(pltpu.make_async_copy(part, place, sems.at[first + step]))
    return copies


def copy_rows(table, target, picks, first, count):
    for start in range(0, count, UNROLL):
        places = range(start, min(start + UNROLL, count))
        rows = [table[pl.ds(picks[first + at], 1), :] for at in places]
        for at, row in zip(places, rows):
            target[at : at + 1, :] = row


def matmul(left, right, left_dim=1, right_dim=0):
    return lax.dot_general(
        left, right, (((left_dim,), (right_dim,)), ((), ())), preferred_element_type=jnp.float32
    )


def pick_halo(lists, part0, part1, part2, part3, out, tile_feats, table, stage, sems):
    tile_rows, channels = tile_feats.shape
    slots = stage.shape[0]
    copies = part_copies((part0, part1, part2, part3), tile_feats, sems, 0)
    for copy in copies:
        copy.start()
    table[pl.ds(tile_rows, 8), :] = jnp.zeros((8, channels), jnp.float32)
    out[...] = jnp.zeros_like(out)
    y, z, core = (lax.axis_index(name) for name in TILE)
    own = (y * DEPTH_Z + z) * CORES + core
    for copy in copies:
        copy.wait()
    table[pl.ds(0, tile_rows), :] = tile_feats[...].astype(jnp.float32)
    planes, lines = RING_X * RING_Y * DEPTH_Z * CORES // (RING_X * GRID_W * GRID_H), GRID_H

    def body(at, carry):
        line = own % (GRID_W * GRID_H) // GRID_W + at // 3 % 3 - 1
        column = own % GRID_W + at % 3 - 1
        inside = (line >= 0) & (line < lines) & (column >= 0) & (column < GRID_W)
        tile = (at // 9 % planes * GRID_H + line) * GRID_W + column
        tile = jnp.where(inside, tile, own)
        first = pl.multiple_of(tile * slots, slots)
        copy_rows(table, stage, lists, first, slots)
        out[pl.ds(first, slots), :] = stage[...].astype(jnp.bfloat16)
        return carry

    lax.fori_loop(0, 9 * planes, body, 0)


def grad_kernel(
    grad0, grad1, grad2, grad3, down_weight, link_column, parent_out, hidden_out, tile_grad, sems
):
    copies = part_copies((grad0, grad1, grad2, grad3), tile_grad, sems, 0)
    for copy in copies:
        copy.start()
    octants = down_weight.shape[0]
    rows, channels = hidden_out.shape
    link = link_column[...]
    octant = link % octants
    columns = lax.broadcasted_iota(jnp.int32, (rows, tile_grad.shape[0]), 1)
    at_parent = ((link // octants) == columns).astype(jnp.bfloat16)
    for copy in copies:
        copy.wait()
    parent_grad = matmul(at_parent, tile_grad[...]).astype(jnp.bfloat16)
    hidden_grad = jnp.zeros((rows, channels), jnp.float32)
    for o in range(octants):
        back = matmul(parent_grad, down_weight[o], 1, 1)
        hidden_grad += jnp.where(octant == o, back, 0.0)
    parent_out[...] = parent_grad
    hidden_out[...] = hidden_grad


def step_kernel(
    kernel_map, part0, part1, part2, part3, incoming, conv_hbm, down_hbm, parent_hbm, back_hbm,
    link_column, link_row,
    coarse, mine, other,
    tile_feats, table, stage, gathered, pre_act, conv_weight, down_weight, parent_grad, back_grad, sems,
):
    rows, channels = part0.shape
    offsets = conv_weight.shape[0]
    octants, _, out_channels = down_weight.shape
    tile_rows, halo_rows = tile_feats.shape[0], incoming.shape[0]
    coarse_tile = coarse.shape[0]
    feats = part_copies((part0, part1, part2, part3), tile_feats, sems, 0)
    conv = pltpu.make_async_copy(conv_hbm, conv_weight, sems.at[4])
    late = [
        pltpu.make_async_copy(down_hbm, down_weight, sems.at[5]),
        pltpu.make_async_copy(parent_hbm, parent_grad, sems.at[6]),
        pltpu.make_async_copy(back_hbm, back_grad, sems.at[7]),
    ]
    for copy in feats + [conv] + late:
        copy.start()
    pre_act[...] = jnp.zeros_like(pre_act)
    table[pl.ds(tile_rows + halo_rows, 8), :] = jnp.zeros((8, channels), jnp.float32)
    table[pl.ds(tile_rows, halo_rows), :] = incoming[...].astype(jnp.float32)
    for copy in feats:
        copy.wait()
    table[pl.ds(0, tile_rows), :] = tile_feats[...].astype(jnp.float32)
    middle = offsets // 2
    own = pl.multiple_of(lax.axis_index("x") * rows, rows)
    gathered[middle] = tile_feats[pl.ds(own, rows), :]
    conv.wait()

    def forward(at, previous):
        offset = at + (at >= middle).astype(jnp.int32)
        pre_act[...] += matmul(gathered[previous], conv_weight[previous])
        copy_rows(table, stage, kernel_map, offset * rows, rows)
        gathered[offset] = stage[...].astype(jnp.bfloat16)
        return offset

    last = lax.fori_loop(0, offsets - 1, forward, jnp.int32(middle))
    for copy in late:
        copy.wait()
    act = pre_act[...] + matmul(gathered[last], conv_weight[last])
    gate = 1.0 / (1.0 + jnp.exp(-act))
    hidden_wide = act * gate
    hidden = hidden_wide.astype(jnp.bfloat16)
    hidden_turned = hidden_wide.T.astype(jnp.bfloat16)
    pre_grad = back_grad[...] * gate * (1.0 + act * (1.0 - gate))
    pre_grad_turned = pre_grad.T.astype(jnp.bfloat16)
    octant = link_column[...] % octants
    link_turned = link_row[...]
    octant_turned = link_turned % octants
    own_term = jnp.zeros((rows, out_channels), jnp.float32)
    for o in range(octants):
        only = jnp.where(octant == o, hidden, jnp.zeros_like(hidden))
        own_term += matmul(only, down_weight[o])
    from_row = (link_turned // octants) == lax.broadcasted_iota(jnp.int32, (coarse_tile, rows), 0)
    from_row = from_row.astype(jnp.bfloat16)
    high = own_term.astype(jnp.bfloat16)
    low = (own_term - high.astype(jnp.float32)).astype(jnp.bfloat16)
    coarse[...] = (matmul(from_row, high) + matmul(from_row, low)).astype(jnp.bfloat16)

    half_blocks = mine.shape[0] // channels
    down_first = offsets - half_blocks

    def fill(first, second):
        def backward(target, start):
            def body(at, carry):
                turned = matmul(pre_grad_turned, gathered[start + at])
                place = pl.ds(pl.multiple_of(at * channels, channels), channels)
                target[place, :] = turned.T.astype(jnp.bfloat16)
                return carry

            return body

        lax.fori_loop(0, half_blocks, backward(first, 0), 0, unroll=2)
        lax.fori_loop(0, down_first, backward(second, half_blocks), 0, unroll=True)
        for o in range(octants):
            only = jnp.where(octant_turned == o, hidden_turned, jnp.zeros_like(hidden_turned))
            product = matmul(only, parent_grad[...]).astype(jnp.bfloat16)
            left, right = (down_first + o) * channels, (down_first + octants + o) * channels
            second[pl.ds(left, channels), :] = product[:, :channels]
            second[pl.ds(right, channels), :] = product[:, channels:]
        used = (down_first + 2 * octants) * channels
        second[pl.ds(used, second.shape[0] - used), :] = jnp.zeros(
            (second.shape[0] - used, channels), jnp.bfloat16
        )

    core = lax.axis_index("core")

    @pl.when(core == 0)
    def _():
        fill(mine, other)

    @pl.when(core == 1)
    def _():
        fill(other, mine)


def shards(features, kernel_map, send_lists, fine_to_coarse, conv_weight, down_weight, coarse_grad):
    rows, channels = features.shape
    tiles, slots = send_lists.shape[2:]
    offsets = kernel_map.shape[0]
    octants, _, out_channels = down_weight.shape
    tile_rows, halo_rows = RING_X * rows, tiles * slots
    coarse_rows = coarse_grad.shape[0]
    coarse_tile = RING_X * coarse_rows
    smem, vmem = pl.BlockSpec(memory_space=pltpu.SMEM), pl.BlockSpec(memory_space=pltpu.VMEM)
    anywhere = pl.BlockSpec(memory_space=pltpu.HBM)
    parts = share_over_x(features)
    outgoing = pl.pallas_call(
        pick_halo,
        out_shape=jax.ShapeDtypeStruct((halo_rows, channels), jnp.bfloat16),
        in_specs=[smem] + [anywhere] * 4,
        out_specs=vmem,
        scratch_shapes=[
            pltpu.VMEM((tile_rows, channels), jnp.bfloat16),
            pltpu.VMEM((tile_rows + 8, channels), jnp.float32),
            pltpu.VMEM((slots, channels), jnp.float32),
            pltpu.SemaphoreType.DMA((4,)),
        ],
        compiler_params=pltpu.CompilerParams(vmem_limit_bytes=56 << 20),
        name="pick_halo",
    )(send_lists.reshape(halo_rows), *parts)
    later_grad, outgoing = lax.optimization_barrier((coarse_grad, outgoing))
    incoming = lax.all_to_all(
        outgoing.reshape(tiles, slots, channels), TILE, split_axis=0, concat_axis=0, tiled=True
    )
    grads = share_over_x(later_grad)
    x = lax.axis_index("x")
    link = lax.dynamic_slice_in_dim(fine_to_coarse, x * rows, rows)
    used = offsets * channels + 2 * octants * channels
    total = used + (-used % 512)
    link_column, link_row = link.reshape(rows, 1), link.reshape(1, rows)
    parent_grad, back_grad = pl.pallas_call(
        grad_kernel,
        out_shape=(
            jax.ShapeDtypeStruct((rows, out_channels), jnp.bfloat16),
            jax.ShapeDtypeStruct((rows, channels), jnp.float32),
        ),
        in_specs=[anywhere] * 4 + [vmem] * 2,
        out_specs=(vmem, vmem),
        scratch_shapes=[
            pltpu.VMEM((coarse_tile, out_channels), jnp.bfloat16),
            pltpu.SemaphoreType.DMA((4,)),
        ],
        compiler_params=pltpu.CompilerParams(vmem_limit_bytes=56 << 20),
        name="coarse_back",
    )(*grads, down_weight, link_column)
    half = total // CORES
    coarse, mine, other = pl.pallas_call(
        step_kernel,
        out_shape=(
            jax.ShapeDtypeStruct((coarse_tile, out_channels), jnp.bfloat16),
            jax.ShapeDtypeStruct((half, channels), jnp.bfloat16),
            jax.ShapeDtypeStruct((half, channels), jnp.bfloat16),
        ),
        in_specs=[smem] + [anywhere] * 4 + [vmem] + [anywhere] * 4 + [vmem] * 2,
        out_specs=(vmem, vmem, vmem),
        scratch_shapes=[
            pltpu.VMEM((tile_rows, channels), jnp.bfloat16),
            pltpu.VMEM((tile_rows + halo_rows + 8, channels), jnp.float32),
            pltpu.VMEM((rows, channels), jnp.float32),
            pltpu.VMEM((offsets, rows, channels), jnp.bfloat16),
            pltpu.VMEM((rows, channels), jnp.float32),
            pltpu.VMEM(conv_weight.shape, jnp.bfloat16),
            pltpu.VMEM(down_weight.shape, jnp.bfloat16),
            pltpu.VMEM((rows, out_channels), jnp.bfloat16),
            pltpu.VMEM((rows, channels), jnp.float32),
            pltpu.SemaphoreType.DMA((8,)),
        ],
        compiler_params=pltpu.CompilerParams(vmem_limit_bytes=56 << 20),
        name="step",
    )(
        kernel_map.reshape(offsets * rows), *parts, incoming.reshape(halo_rows, channels),
        conv_weight, down_weight, parent_grad, back_grad, link_column, link_row,
    )
    sums, coarse_out = sum_over_devices(mine, other, coarse)
    conv_grad = sums[: offsets * channels].reshape(offsets, channels, channels)
    down_sums = sums[offsets * channels : used]
    half = octants * channels
    down_grad = jnp.concatenate([down_sums[:half], down_sums[half:]], axis=1)
    down_grad = down_grad.reshape(octants, channels, out_channels)
    return (coarse_out, conv_grad, down_grad)


def solution(mesh):
    fine_mesh = Mesh(mesh.devices.reshape(RING_Y, DEPTH_Z, CORES, RING_X), AXES)
    placed = (
        P(AXES, None),
        P(None, AXES),
        P(TILE, "x", None, None),
        P(TILE),
        P(),
        P(),
        P(AXES, None),
    )
    return jax.shard_map(
        shards,
        mesh=fine_mesh,
        in_specs=placed,
        out_specs=(P(AXES, None), P(), P()),
        check_vma=False,
    )
```

```python
import jax
import jax.numpy as jnp
from jax import lax
from jax.experimental import pallas as pl
from jax.experimental.pallas import tpu as pltpu
from jax.sharding import Mesh, PartitionSpec as P

RING_Y, DEPTH_Z, CORES, RING_X = 4, 8, 2, 4
AXES = ("y", "z", "core", "x")
TILE = ("y", "z", "core")
UNROLL = 32
GRID_W, GRID_H = 8, 4


def device_index(place):
    tile = (place[0] * DEPTH_Z + place[1]) * CORES + place[2]
    return tile * RING_X + place[3]


def partner_pairs(partner):
    pairs = []
    for y in range(RING_Y):
        for z in range(DEPTH_Z):
            for core in range(CORES):
                for x in range(RING_X):
                    place = (y, z, core, x)
                    pairs.append((device_index(place), device_index(partner(*place))))
    return pairs


def send(value, partner):
    return lax.ppermute(value, AXES, partner_pairs(partner))


def across_core(y, z, core, x):
    return (y, z, 1 - core, x)


def square(step, hop):
    def partner(y, z, core, x):
        return (y ^ (hop if step & 2 else 0), z, core, x ^ (hop if step & 1 else 0))

    return partner


def first_ring(step):
    return lambda y, z, core, x: square(step, 1 if core else 3)(y, z, core, x)


def second_ring(step):
    return lambda y, z, core, x: square(step, 3 if core else 1)(y, z, core, x)


def along_z(step):
    return lambda y, z, core, x: (y, z ^ step, core, x)


def narrow(value):
    return value.astype(jnp.bfloat16)


def wide(value):
    return value.astype(jnp.float32)


def pick(parts, digit):
    return lax.dynamic_index_in_dim(parts, digit, 0, keepdims=False)


def scatter_ring(parts, digit, ring, extra):
    rows = parts.shape[1]
    first = jnp.concatenate([pick(parts, digit ^ 1), extra], axis=0)
    first = send(first, ring(1))
    received = [first[:rows]] + [send(pick(parts, digit ^ step), ring(step)) for step in (2, 3)]
    total = wide(pick(parts, digit))
    for part in received:
        total = total + wide(part)
    return narrow(total), first[rows:]


def swap(first, second, flip):
    return jnp.where(flip, second, first), jnp.where(flip, first, second)


def gather_pair(part, digit, partner):
    other = send(part, partner)
    return jnp.stack(swap(part, other, digit == 1))


def gather_ring(part, digit, ring):
    parts = [part] + [send(part, ring(step)) for step in (1, 2, 3)]
    low, high = digit % 2 == 1, digit // 2 == 1
    first, second = swap(parts[0], parts[1], low)
    third, fourth = swap(parts[2], parts[3], low)
    first, third = swap(first, third, high)
    second, fourth = swap(second, fourth, high)
    return jnp.stack([first, second, third, fourth])


def sum_over_devices(mine, other, coarse):
    y, z, core, x = (lax.axis_index(name) for name in AXES)
    near_x, near_y = (x ^ (x >> 1)) & 1, (y ^ (y >> 1)) & 1
    far_x, far_y = x >> 1, y >> 1
    near, far = near_x + 2 * near_y, far_x + 2 * far_y
    ring_one = jnp.where(core == 0, far, near)
    ring_two = jnp.where(core == 0, near, far)
    rows, lanes = mine.shape[0] // (RING_X * RING_Y), mine.shape[1]
    part = narrow(wide(mine) + wide(send(other, across_core)))
    hop_one, hop_two = jnp.where(core == 0, 3, 1), jnp.where(core == 0, 1, 3)
    quarters = coarse.reshape(RING_X, coarse.shape[0] // RING_X, lanes)
    extra = jnp.concatenate([pick(quarters, x ^ hop_one), pick(quarters, x ^ 2)], axis=0)
    part, extra = scatter_ring(part.reshape(4, 4 * rows, lanes), ring_one, first_ring, extra)
    quarter = quarters.shape[1]
    kept = wide(pick(quarters, x)) + wide(extra[:quarter])
    passed = narrow(wide(pick(quarters, x ^ hop_two)) + wide(extra[quarter:]))
    part, extra = scatter_ring(part.reshape(4, rows, lanes), ring_two, second_ring, passed)
    halves = narrow(kept + wide(extra)).reshape(2, quarter // 2, lanes)
    coarse_out = jnp.concatenate([halves[0], halves[1]], axis=1)
    for step in (1, 2, 7):
        part = narrow(wide(part) + wide(send(part, along_z(step))))
    part = gather_ring(part, ring_two, second_ring).reshape(RING_Y * rows, lanes)
    part = gather_ring(part, ring_one, first_ring).reshape(RING_X * RING_Y * rows, lanes)
    return wide(gather_pair(part, core, across_core)).reshape(-1, lanes), coarse_out


def ring_x(step):
    return lambda y, z, core, x: (y, z, core, x ^ step)


def share_over_x(value):
    return [value] + [send(value, ring_x(step)) for step in (1, 2, 3)]


def part_copies(parts, target, sems, first):
    x = lax.axis_index("x")
    rows = parts[0].shape[0]
    copies = []
    for step, part in enumerate(parts):
        place = target.at[pl.ds(pl.multiple_of((x ^ step) * rows, rows), rows)]
        copies.append(pltpu.make_async_copy(part, place, sems.at[first + step]))
    return copies


def copy_rows(table, target, picks, first, count):
    for start in range(0, count, UNROLL):
        places = range(start, min(start + UNROLL, count))
        rows = [table[pl.ds(picks[first + at], 1), :] for at in places]
        for at, row in zip(places, rows):
            target[at : at + 1, :] = row


def matmul(left, right, left_dim=1, right_dim=0):
    return lax.dot_general(
        left, right, (((left_dim,), (right_dim,)), ((), ())), preferred_element_type=jnp.float32
    )


def pick_halo(lists, part0, part1, part2, part3, out, tile_feats, table, stage, sems):
    tile_rows, channels = tile_feats.shape
    slots = stage.shape[0]
    copies = part_copies((part0, part1, part2, part3), tile_feats, sems, 0)
    for copy in copies:
        copy.start()
    table[pl.ds(tile_rows, 8), :] = jnp.zeros((8, channels), jnp.float32)
    out[...] = jnp.zeros_like(out)
    y, z, core = (lax.axis_index(name) for name in TILE)
    own = (y * DEPTH_Z + z) * CORES + core
    for copy in copies:
        copy.wait()
    table[pl.ds(0, tile_rows), :] = tile_feats[...].astype(jnp.float32)
    planes, lines = RING_X * RING_Y * DEPTH_Z * CORES // (RING_X * GRID_W * GRID_H), GRID_H

    def body(at, carry):
        line = own % (GRID_W * GRID_H) // GRID_W + at // 3 % 3 - 1
        column = own % GRID_W + at % 3 - 1
        inside = (line >= 0) & (line < lines) & (column >= 0) & (column < GRID_W)
        tile = (at // 9 % planes * GRID_H + line) * GRID_W + column
        tile = jnp.where(inside, tile, own)
        first = pl.multiple_of(tile * slots, slots)
        copy_rows(table, stage, lists, first, slots)
        out[pl.ds(first, slots), :] = stage[...].astype(jnp.bfloat16)
        return carry

    lax.fori_loop(0, 9 * planes, body, 0)


def grad_kernel(
    grad0, grad1, grad2, grad3, down_weight, link_column, parent_out, hidden_out, tile_grad, sems
):
    copies = part_copies((grad0, grad1, grad2, grad3), tile_grad, sems, 0)
    for copy in copies:
        copy.start()
    octants = down_weight.shape[0]
    rows, channels = hidden_out.shape
    link = link_column[...]
    octant = link % octants
    columns = lax.broadcasted_iota(jnp.int32, (rows, tile_grad.shape[0]), 1)
    at_parent = ((link // octants) == columns).astype(jnp.bfloat16)
    for copy in copies:
        copy.wait()
    parent_grad = matmul(at_parent, tile_grad[...]).astype(jnp.bfloat16)
    hidden_grad = jnp.zeros((rows, channels), jnp.float32)
    for o in range(octants):
        back = matmul(parent_grad, down_weight[o], 1, 1)
        hidden_grad += jnp.where(octant == o, back, 0.0)
    parent_out[...] = parent_grad
    hidden_out[...] = hidden_grad


def step_kernel(
    kernel_map, part0, part1, part2, part3, incoming, conv_hbm, down_hbm, parent_hbm, back_hbm,
    link_column, link_row,
    coarse, mine, other,
    tile_feats, table, stage, gathered, pre_act, conv_weight, down_weight, parent_grad, back_grad, sems,
):
    rows, channels = part0.shape
    offsets = conv_weight.shape[0]
    octants, _, out_channels = down_weight.shape
    tile_rows, halo_rows = tile_feats.shape[0], incoming.shape[0]
    coarse_tile = coarse.shape[0] * channels // out_channels
    feats = part_copies((part0, part1, part2, part3), tile_feats, sems, 0)
    conv = pltpu.make_async_copy(conv_hbm, conv_weight, sems.at[4])
    late = [
        pltpu.make_async_copy(down_hbm, down_weight, sems.at[5]),
        pltpu.make_async_copy(parent_hbm, parent_grad, sems.at[6]),
        pltpu.make_async_copy(back_hbm, back_grad, sems.at[7]),
    ]
    for copy in feats + [conv] + late:
        copy.start()
    pre_act[...] = jnp.zeros_like(pre_act)
    table[pl.ds(tile_rows + halo_rows, 8), :] = jnp.zeros((8, channels), jnp.float32)
    table[pl.ds(tile_rows, halo_rows), :] = incoming[...].astype(jnp.float32)
    for copy in feats:
        copy.wait()
    table[pl.ds(0, tile_rows), :] = tile_feats[...].astype(jnp.float32)
    middle = offsets // 2
    own = pl.multiple_of(lax.axis_index("x") * rows, rows)
    gathered[middle] = tile_feats[pl.ds(own, rows), :]
    conv.wait()

    def forward(at, previous):
        offset = at + (at >= middle).astype(jnp.int32)
        pre_act[...] += matmul(gathered[previous], conv_weight[previous])
        copy_rows(table, stage, kernel_map, offset * rows, rows)
        gathered[offset] = stage[...].astype(jnp.bfloat16)
        return offset

    last = lax.fori_loop(0, offsets - 1, forward, jnp.int32(middle))
    for copy in late:
        copy.wait()
    act = pre_act[...] + matmul(gathered[last], conv_weight[last])
    gate = 1.0 / (1.0 + jnp.exp(-act))
    hidden_wide = act * gate
    hidden = hidden_wide.astype(jnp.bfloat16)
    hidden_turned = hidden_wide.T.astype(jnp.bfloat16)
    pre_grad = back_grad[...] * gate * (1.0 + act * (1.0 - gate))
    pre_grad_turned = pre_grad.T.astype(jnp.bfloat16)
    octant = link_column[...] % octants
    link_turned = link_row[...]
    octant_turned = link_turned % octants
    own_term = jnp.zeros((rows, out_channels), jnp.float32)
    for o in range(octants):
        only = jnp.where(octant == o, hidden, jnp.zeros_like(hidden))
        own_term += matmul(only, down_weight[o])
    from_row = (link_turned // octants) == lax.broadcasted_iota(jnp.int32, (coarse_tile, rows), 0)
    from_row = from_row.astype(jnp.bfloat16)
    high = own_term.astype(jnp.bfloat16)
    low = (own_term - high.astype(jnp.float32)).astype(jnp.bfloat16)
    coarse_sums = (matmul(from_row, high) + matmul(from_row, low)).astype(jnp.bfloat16)
    quarter = coarse_tile // RING_X
    for at in range(2 * RING_X):
        block = coarse_sums[at // 2 * quarter : (at // 2 + 1) * quarter]
        block = block[:, at % 2 * channels : (at % 2 + 1) * channels]
        coarse[pl.ds(at * quarter, quarter), :] = block

    half_blocks = mine.shape[0] // channels
    down_first = offsets - half_blocks

    def fill(first, second):
        def backward(target, start):
            def body(at, carry):
                turned = matmul(pre_grad_turned, gathered[start + at])
                place = pl.ds(pl.multiple_of(at * channels, channels), channels)
                target[place, :] = turned.T.astype(jnp.bfloat16)
                return carry

            return body

        lax.fori_loop(0, half_blocks, backward(first, 0), 0, unroll=2)
        lax.fori_loop(0, down_first, backward(second, half_blocks), 0, unroll=True)
        for o in range(octants):
            only = jnp.where(octant_turned == o, hidden_turned, jnp.zeros_like(hidden_turned))
            product = matmul(only, parent_grad[...]).astype(jnp.bfloat16)
            left, right = (down_first + o) * channels, (down_first + octants + o) * channels
            second[pl.ds(left, channels), :] = product[:, :channels]
            second[pl.ds(right, channels), :] = product[:, channels:]
        used = (down_first + 2 * octants) * channels
        second[pl.ds(used, second.shape[0] - used), :] = jnp.zeros(
            (second.shape[0] - used, channels), jnp.bfloat16
        )

    core = lax.axis_index("core")

    @pl.when(core == 0)
    def _():
        fill(mine, other)

    @pl.when(core == 1)
    def _():
        fill(other, mine)


def shards(features, kernel_map, send_lists, fine_to_coarse, conv_weight, down_weight, coarse_grad):
    rows, channels = features.shape
    tiles, slots = send_lists.shape[2:]
    offsets = kernel_map.shape[0]
    octants, _, out_channels = down_weight.shape
    tile_rows, halo_rows = RING_X * rows, tiles * slots
    coarse_rows = coarse_grad.shape[0]
    coarse_tile = RING_X * coarse_rows
    smem, vmem = pl.BlockSpec(memory_space=pltpu.SMEM), pl.BlockSpec(memory_space=pltpu.VMEM)
    anywhere = pl.BlockSpec(memory_space=pltpu.HBM)
    parts = share_over_x(features)
    outgoing = pl.pallas_call(
        pick_halo,
        out_shape=jax.ShapeDtypeStruct((halo_rows, channels), jnp.bfloat16),
        in_specs=[smem] + [anywhere] * 4,
        out_specs=vmem,
        scratch_shapes=[
            pltpu.VMEM((tile_rows, channels), jnp.bfloat16),
            pltpu.VMEM((tile_rows + 8, channels), jnp.float32),
            pltpu.VMEM((slots, channels), jnp.float32),
            pltpu.SemaphoreType.DMA((4,)),
        ],
        compiler_params=pltpu.CompilerParams(vmem_limit_bytes=56 << 20),
        name="pick_halo",
    )(send_lists.reshape(halo_rows), *parts)
    later_grad, outgoing = lax.optimization_barrier((coarse_grad, outgoing))
    incoming = lax.all_to_all(
        outgoing.reshape(tiles, slots, channels), TILE, split_axis=0, concat_axis=0, tiled=True
    )
    grads = share_over_x(later_grad)
    x = lax.axis_index("x")
    link = lax.dynamic_slice_in_dim(fine_to_coarse, x * rows, rows)
    used = offsets * channels + 2 * octants * channels
    total = used + (-used % 512)
    link_column, link_row = link.reshape(rows, 1), link.reshape(1, rows)
    parent_grad, back_grad = pl.pallas_call(
        grad_kernel,
        out_shape=(
            jax.ShapeDtypeStruct((rows, out_channels), jnp.bfloat16),
            jax.ShapeDtypeStruct((rows, channels), jnp.float32),
        ),
        in_specs=[anywhere] * 4 + [vmem] * 2,
        out_specs=(vmem, vmem),
        scratch_shapes=[
            pltpu.VMEM((coarse_tile, out_channels), jnp.bfloat16),
            pltpu.SemaphoreType.DMA((4,)),
        ],
        compiler_params=pltpu.CompilerParams(vmem_limit_bytes=56 << 20),
        name="coarse_back",
    )(*grads, down_weight, link_column)
    half = total // CORES
    coarse, mine, other = pl.pallas_call(
        step_kernel,
        out_shape=(
            jax.ShapeDtypeStruct((coarse_tile * out_channels // channels, channels), jnp.bfloat16),
            jax.ShapeDtypeStruct((half, channels), jnp.bfloat16),
            jax.ShapeDtypeStruct((half, channels), jnp.bfloat16),
        ),
        in_specs=[smem] + [anywhere] * 4 + [vmem] + [anywhere] * 4 + [vmem] * 2,
        out_specs=(vmem, vmem, vmem),
        scratch_shapes=[
            pltpu.VMEM((tile_rows, channels), jnp.bfloat16),
            pltpu.VMEM((tile_rows + halo_rows + 8, channels), jnp.float32),
            pltpu.VMEM((rows, channels), jnp.float32),
            pltpu.VMEM((offsets, rows, channels), jnp.bfloat16),
            pltpu.VMEM((rows, channels), jnp.float32),
            pltpu.VMEM(conv_weight.shape, jnp.bfloat16),
            pltpu.VMEM(down_weight.shape, jnp.bfloat16),
            pltpu.VMEM((rows, out_channels), jnp.bfloat16),
            pltpu.VMEM((rows, channels), jnp.float32),
            pltpu.SemaphoreType.DMA((8,)),
        ],
        compiler_params=pltpu.CompilerParams(vmem_limit_bytes=56 << 20),
        name="step",
    )(
        kernel_map.reshape(offsets * rows), *parts, incoming.reshape(halo_rows, channels),
        conv_weight, down_weight, parent_grad, back_grad, link_column, link_row,
    )
    sums, coarse_out = sum_over_devices(mine, other, coarse)
    conv_grad = sums[: offsets * channels].reshape(offsets, channels, channels)
    down_sums = sums[offsets * channels : used]
    half = octants * channels
    down_grad = jnp.concatenate([down_sums[:half], down_sums[half:]], axis=1)
    down_grad = down_grad.reshape(octants, channels, out_channels)
    return (coarse_out, conv_grad, down_grad)


def solution(mesh):
    fine_mesh = Mesh(mesh.devices.reshape(RING_Y, DEPTH_Z, CORES, RING_X), AXES)
    placed = (
        P(AXES, None),
        P(None, AXES),
        P(TILE, "x", None, None),
        P(TILE),
        P(),
        P(),
        P(AXES, None),
    )
    return jax.shard_map(
        shards,
        mesh=fine_mesh,
        in_specs=placed,
        out_specs=(P(AXES, None), P(), P()),
        check_vma=False,
    )
```

```python
import jax
import jax.numpy as jnp
from jax import lax
from jax.experimental import pallas as pl
from jax.experimental.pallas import tpu as pltpu
from jax.sharding import Mesh, PartitionSpec as P

RING_Y, DEPTH_Z, CORES, RING_X = 4, 8, 2, 4
AXES = ("y", "z", "core", "x")
TILE = ("y", "z", "core")
UNROLL = 32
GRID_W, GRID_H = 8, 4


def device_index(place):
    tile = (place[0] * DEPTH_Z + place[1]) * CORES + place[2]
    return tile * RING_X + place[3]


def partner_pairs(partner):
    pairs = []
    for y in range(RING_Y):
        for z in range(DEPTH_Z):
            for core in range(CORES):
                for x in range(RING_X):
                    place = (y, z, core, x)
                    pairs.append((device_index(place), device_index(partner(*place))))
    return pairs


def send(value, partner):
    return lax.ppermute(value, AXES, partner_pairs(partner))


def across_core(y, z, core, x):
    return (y, z, 1 - core, x)


def square(step, hop):
    def partner(y, z, core, x):
        return (y ^ (hop if step & 2 else 0), z, core, x ^ (hop if step & 1 else 0))

    return partner


def first_ring(step):
    return lambda y, z, core, x: square(step, 1 if core else 3)(y, z, core, x)


def second_ring(step):
    return lambda y, z, core, x: square(step, 3 if core else 1)(y, z, core, x)


def along_z(step):
    return lambda y, z, core, x: (y, z ^ step, core, x)


def narrow(value):
    return value.astype(jnp.bfloat16)


def wide(value):
    return value.astype(jnp.float32)


def pick(parts, digit):
    return lax.dynamic_index_in_dim(parts, digit, 0, keepdims=False)


def scatter_ring(parts, digit, ring, extra):
    rows = parts.shape[1]
    first = jnp.concatenate([pick(parts, digit ^ 1), extra], axis=0)
    first = send(first, ring(1))
    received = [first[:rows]] + [send(pick(parts, digit ^ step), ring(step)) for step in (2, 3)]
    total = wide(pick(parts, digit))
    for part in received:
        total = total + wide(part)
    return narrow(total), first[rows:]


def swap(first, second, flip):
    return jnp.where(flip, second, first), jnp.where(flip, first, second)


def gather_pair(part, digit, partner):
    other = send(part, partner)
    return jnp.stack(swap(part, other, digit == 1))


def gather_ring(part, digit, ring):
    parts = [part] + [send(part, ring(step)) for step in (1, 2, 3)]
    low, high = digit % 2 == 1, digit // 2 == 1
    first, second = swap(parts[0], parts[1], low)
    third, fourth = swap(parts[2], parts[3], low)
    first, third = swap(first, third, high)
    second, fourth = swap(second, fourth, high)
    return jnp.stack([first, second, third, fourth])


def sum_over_devices(mine, other, coarse):
    y, z, core, x = (lax.axis_index(name) for name in AXES)
    near_x, near_y = (x ^ (x >> 1)) & 1, (y ^ (y >> 1)) & 1
    far_x, far_y = x >> 1, y >> 1
    near, far = near_x + 2 * near_y, far_x + 2 * far_y
    ring_one = jnp.where(core == 0, far, near)
    ring_two = jnp.where(core == 0, near, far)
    rows, lanes = mine.shape[0] // (RING_X * RING_Y), mine.shape[1]
    part = narrow(wide(mine) + wide(send(other, across_core)))
    hop_one, hop_two = jnp.where(core == 0, 3, 1), jnp.where(core == 0, 1, 3)
    quarters = coarse.reshape(RING_X, coarse.shape[0] // RING_X, lanes)
    extra = jnp.concatenate([pick(quarters, x ^ hop_one), pick(quarters, x ^ 2)], axis=0)
    part, extra = scatter_ring(part.reshape(4, 4 * rows, lanes), ring_one, first_ring, extra)
    quarter = quarters.shape[1]
    kept = wide(pick(quarters, x)) + wide(extra[:quarter])
    passed = narrow(wide(pick(quarters, x ^ hop_two)) + wide(extra[quarter:]))
    part, extra = scatter_ring(part.reshape(4, rows, lanes), ring_two, second_ring, passed)
    halves = narrow(kept + wide(extra)).reshape(2, quarter // 2, lanes)
    coarse_out = jnp.concatenate([halves[0], halves[1]], axis=1)
    for step in (1, 2, 7):
        part = narrow(wide(part) + wide(send(part, along_z(step))))
    part = gather_ring(part, ring_two, second_ring).reshape(RING_Y * rows, lanes)
    part = gather_ring(part, ring_one, first_ring).reshape(RING_X * RING_Y * rows, lanes)
    return wide(gather_pair(part, core, across_core)).reshape(-1, lanes), coarse_out


def ring_x(step):
    return lambda y, z, core, x: (y, z, core, x ^ step)


def share_over_x(value):
    return [value] + [send(value, ring_x(step)) for step in (1, 2, 3)]


def part_copies(parts, target, sems, first):
    x = lax.axis_index("x")
    rows = parts[0].shape[0]
    copies = []
    for step, part in enumerate(parts):
        place = target.at[pl.ds(pl.multiple_of((x ^ step) * rows, rows), rows)]
        copies.append(pltpu.make_async_copy(part, place, sems.at[first + step]))
    return copies


def copy_rows(table, target, picks, first, count):
    for start in range(0, count, UNROLL):
        places = range(start, min(start + UNROLL, count))
        rows = [table[pl.ds(picks[first + at], 1), :] for at in places]
        for at, row in zip(places, rows):
            target[at : at + 1, :] = row


def copy_pairs(table, target, words, first, count):
    half = count // 2
    for start in range(0, half, UNROLL // 2):
        rows = []
        for at in range(start, start + UNROLL // 2):
            word = words[first + at]
            rows.append((at, table[pl.ds(word & 0xFFFF, 1), :]))
            rows.append((half + at, table[pl.ds(lax.shift_right_logical(word, 16), 1), :]))
        for at, row in rows:
            target[at : at + 1, :] = row


def matmul(left, right, left_dim=1, right_dim=0):
    return lax.dot_general(
        left, right, (((left_dim,), (right_dim,)), ((), ())), preferred_element_type=jnp.float32
    )


def pick_halo(lists, part0, part1, part2, part3, out, tile_feats, table, stage, sems):
    tile_rows, channels = tile_feats.shape
    slots = stage.shape[0]
    copies = part_copies((part0, part1, part2, part3), tile_feats, sems, 0)
    for copy in copies:
        copy.start()
    table[pl.ds(tile_rows, 8), :] = jnp.zeros((8, channels), jnp.float32)
    out[...] = jnp.zeros_like(out)
    y, z, core = (lax.axis_index(name) for name in TILE)
    own = (y * DEPTH_Z + z) * CORES + core
    for copy in copies:
        copy.wait()
    table[pl.ds(0, tile_rows), :] = tile_feats[...].astype(jnp.float32)
    planes, lines = RING_X * RING_Y * DEPTH_Z * CORES // (RING_X * GRID_W * GRID_H), GRID_H

    def body(at, carry):
        line = own % (GRID_W * GRID_H) // GRID_W + at // 3 % 3 - 1
        column = own % GRID_W + at % 3 - 1
        inside = (line >= 0) & (line < lines) & (column >= 0) & (column < GRID_W)
        tile = (at // 9 % planes * GRID_H + line) * GRID_W + column
        tile = jnp.where(inside, tile, own)
        first = pl.multiple_of(tile * slots, slots)
        copy_rows(table, stage, lists, first, slots)
        out[pl.ds(first, slots), :] = stage[...].astype(jnp.bfloat16)
        return carry

    lax.fori_loop(0, 9 * planes, body, 0)


def grad_kernel(
    grad0, grad1, grad2, grad3, down_weight, link_column, parent_out, hidden_out, tile_grad, sems
):
    copies = part_copies((grad0, grad1, grad2, grad3), tile_grad, sems, 0)
    for copy in copies:
        copy.start()
    octants = down_weight.shape[0]
    rows, channels = hidden_out.shape
    link = link_column[...]
    octant = link % octants
    columns = lax.broadcasted_iota(jnp.int32, (rows, tile_grad.shape[0]), 1)
    at_parent = ((link // octants) == columns).astype(jnp.bfloat16)
    for copy in copies:
        copy.wait()
    parent_grad = matmul(at_parent, tile_grad[...]).astype(jnp.bfloat16)
    hidden_grad = jnp.zeros((rows, channels), jnp.float32)
    for o in range(octants):
        back = matmul(parent_grad, down_weight[o], 1, 1)
        hidden_grad += jnp.where(octant == o, back, 0.0)
    parent_out[...] = parent_grad
    hidden_out[...] = hidden_grad


def step_kernel(
    kernel_map, part0, part1, part2, part3, incoming, conv_hbm, down_hbm, parent_hbm, back_hbm,
    link_column, link_row,
    coarse, mine, other,
    tile_feats, table, stage, gathered, pre_act, conv_weight, down_weight, parent_grad, back_grad, sems,
):
    rows, channels = part0.shape
    offsets = conv_weight.shape[0]
    octants, _, out_channels = down_weight.shape
    tile_rows, halo_rows = tile_feats.shape[0], incoming.shape[0]
    coarse_tile = coarse.shape[0] * channels // out_channels
    feats = part_copies((part0, part1, part2, part3), tile_feats, sems, 0)
    conv = pltpu.make_async_copy(conv_hbm, conv_weight, sems.at[4])
    late = [
        pltpu.make_async_copy(down_hbm, down_weight, sems.at[5]),
        pltpu.make_async_copy(parent_hbm, parent_grad, sems.at[6]),
        pltpu.make_async_copy(back_hbm, back_grad, sems.at[7]),
    ]
    for copy in feats + [conv] + late:
        copy.start()
    pre_act[...] = jnp.zeros_like(pre_act)
    table[pl.ds(tile_rows + halo_rows, 8), :] = jnp.zeros((8, channels), jnp.float32)
    table[pl.ds(tile_rows, halo_rows), :] = incoming[...].astype(jnp.float32)
    for copy in feats:
        copy.wait()
    table[pl.ds(0, tile_rows), :] = tile_feats[...].astype(jnp.float32)
    middle = offsets // 2
    own = pl.multiple_of(lax.axis_index("x") * rows, rows)
    gathered[middle] = tile_feats[pl.ds(own, rows), :]
    conv.wait()

    def forward(at, previous):
        offset = at + (at >= middle).astype(jnp.int32)
        pre_act[...] += matmul(gathered[previous], conv_weight[previous])
        copy_pairs(table, stage, kernel_map, offset * (rows // 2), rows)
        gathered[offset] = stage[...].astype(jnp.bfloat16)
        return offset

    last = lax.fori_loop(0, offsets - 1, forward, jnp.int32(middle))
    for copy in late:
        copy.wait()
    act = pre_act[...] + matmul(gathered[last], conv_weight[last])
    gate = 1.0 / (1.0 + jnp.exp(-act))
    hidden_wide = act * gate
    hidden = hidden_wide.astype(jnp.bfloat16)
    hidden_turned = hidden_wide.T.astype(jnp.bfloat16)
    pre_grad = back_grad[...] * gate * (1.0 + act * (1.0 - gate))
    pre_grad_turned = pre_grad.T.astype(jnp.bfloat16)
    octant = link_column[...] % octants
    link_turned = link_row[...]
    octant_turned = link_turned % octants
    own_term = jnp.zeros((rows, out_channels), jnp.float32)
    for o in range(octants):
        only = jnp.where(octant == o, hidden, jnp.zeros_like(hidden))
        own_term += matmul(only, down_weight[o])
    from_row = (link_turned // octants) == lax.broadcasted_iota(jnp.int32, (coarse_tile, rows), 0)
    from_row = from_row.astype(jnp.bfloat16)
    high = own_term.astype(jnp.bfloat16)
    low = (own_term - high.astype(jnp.float32)).astype(jnp.bfloat16)
    coarse_sums = (matmul(from_row, high) + matmul(from_row, low)).astype(jnp.bfloat16)
    quarter = coarse_tile // RING_X
    for at in range(2 * RING_X):
        block = coarse_sums[at // 2 * quarter : (at // 2 + 1) * quarter]
        block = block[:, at % 2 * channels : (at % 2 + 1) * channels]
        coarse[pl.ds(at * quarter, quarter), :] = block

    half_blocks = mine.shape[0] // channels
    down_first = offsets - half_blocks

    def fill(first, second):
        def backward(target, start):
            def body(at, carry):
                turned = matmul(pre_grad_turned, gathered[start + at])
                place = pl.ds(pl.multiple_of(at * channels, channels), channels)
                target[place, :] = turned.T.astype(jnp.bfloat16)
                return carry

            return body

        lax.fori_loop(0, half_blocks, backward(first, 0), 0, unroll=11)
        lax.fori_loop(0, down_first, backward(second, half_blocks), 0, unroll=True)
        for o in range(octants):
            only = jnp.where(octant_turned == o, hidden_turned, jnp.zeros_like(hidden_turned))
            product = matmul(only, parent_grad[...]).astype(jnp.bfloat16)
            left, right = (down_first + o) * channels, (down_first + octants + o) * channels
            second[pl.ds(left, channels), :] = product[:, :channels]
            second[pl.ds(right, channels), :] = product[:, channels:]
        used = (down_first + 2 * octants) * channels
        second[pl.ds(used, second.shape[0] - used), :] = jnp.zeros(
            (second.shape[0] - used, channels), jnp.bfloat16
        )

    core = lax.axis_index("core")

    @pl.when(core == 0)
    def _():
        fill(mine, other)

    @pl.when(core == 1)
    def _():
        fill(other, mine)


def shards(features, kernel_map, send_lists, fine_to_coarse, conv_weight, down_weight, coarse_grad):
    rows, channels = features.shape
    tiles, slots = send_lists.shape[2:]
    offsets = kernel_map.shape[0]
    octants, _, out_channels = down_weight.shape
    tile_rows, halo_rows = RING_X * rows, tiles * slots
    coarse_rows = coarse_grad.shape[0]
    coarse_tile = RING_X * coarse_rows
    smem, vmem = pl.BlockSpec(memory_space=pltpu.SMEM), pl.BlockSpec(memory_space=pltpu.VMEM)
    anywhere = pl.BlockSpec(memory_space=pltpu.HBM)
    parts = share_over_x(features)
    outgoing = pl.pallas_call(
        pick_halo,
        out_shape=jax.ShapeDtypeStruct((halo_rows, channels), jnp.bfloat16),
        in_specs=[smem] + [anywhere] * 4,
        out_specs=vmem,
        scratch_shapes=[
            pltpu.VMEM((tile_rows, channels), jnp.bfloat16),
            pltpu.VMEM((tile_rows + 8, channels), jnp.float32),
            pltpu.VMEM((slots, channels), jnp.float32),
            pltpu.SemaphoreType.DMA((4,)),
        ],
        compiler_params=pltpu.CompilerParams(vmem_limit_bytes=56 << 20),
        name="pick_halo",
    )(send_lists.reshape(halo_rows), *parts)
    later_grad, outgoing = lax.optimization_barrier((coarse_grad, outgoing))
    incoming = lax.all_to_all(
        outgoing.reshape(tiles, slots, channels), TILE, split_axis=0, concat_axis=0, tiled=True
    )
    grads = share_over_x(later_grad)
    x = lax.axis_index("x")
    link = lax.dynamic_slice_in_dim(fine_to_coarse, x * rows, rows)
    used = offsets * channels + 2 * octants * channels
    total = used + (-used % 512)
    link_column, link_row = link.reshape(rows, 1), link.reshape(1, rows)
    parent_grad, back_grad = pl.pallas_call(
        grad_kernel,
        out_shape=(
            jax.ShapeDtypeStruct((rows, out_channels), jnp.bfloat16),
            jax.ShapeDtypeStruct((rows, channels), jnp.float32),
        ),
        in_specs=[anywhere] * 4 + [vmem] * 2,
        out_specs=(vmem, vmem),
        scratch_shapes=[
            pltpu.VMEM((coarse_tile, out_channels), jnp.bfloat16),
            pltpu.SemaphoreType.DMA((4,)),
        ],
        compiler_params=pltpu.CompilerParams(vmem_limit_bytes=56 << 20),
        name="coarse_back",
    )(*grads, down_weight, link_column)
    half = total // CORES
    map_pairs = kernel_map[:, : rows // 2] | (kernel_map[:, rows // 2 :] << 16)
    map_pairs = map_pairs.reshape(offsets * rows // 2)
    coarse, mine, other = pl.pallas_call(
        step_kernel,
        out_shape=(
            jax.ShapeDtypeStruct((coarse_tile * out_channels // channels, channels), jnp.bfloat16),
            jax.ShapeDtypeStruct((half, channels), jnp.bfloat16),
            jax.ShapeDtypeStruct((half, channels), jnp.bfloat16),
        ),
        in_specs=[smem] + [anywhere] * 4 + [vmem] + [anywhere] * 4 + [vmem] * 2,
        out_specs=(vmem, vmem, vmem),
        scratch_shapes=[
            pltpu.VMEM((tile_rows, channels), jnp.bfloat16),
            pltpu.VMEM((tile_rows + halo_rows + 8, channels), jnp.float32),
            pltpu.VMEM((rows, channels), jnp.float32),
            pltpu.VMEM((offsets, rows, channels), jnp.bfloat16),
            pltpu.VMEM((rows, channels), jnp.float32),
            pltpu.VMEM(conv_weight.shape, jnp.bfloat16),
            pltpu.VMEM(down_weight.shape, jnp.bfloat16),
            pltpu.VMEM((rows, out_channels), jnp.bfloat16),
            pltpu.VMEM((rows, channels), jnp.float32),
            pltpu.SemaphoreType.DMA((8,)),
        ],
        compiler_params=pltpu.CompilerParams(vmem_limit_bytes=56 << 20),
        name="step",
    )(
        map_pairs, *parts, incoming.reshape(halo_rows, channels),
        conv_weight, down_weight, parent_grad, back_grad, link_column, link_row,
    )
    sums, coarse_out = sum_over_devices(mine, other, coarse)
    conv_grad = sums[: offsets * channels].reshape(offsets, channels, channels)
    down_sums = sums[offsets * channels : used]
    half = octants * channels
    down_grad = jnp.concatenate([down_sums[:half], down_sums[half:]], axis=1)
    down_grad = down_grad.reshape(octants, channels, out_channels)
    return (coarse_out, conv_grad, down_grad)


def solution(mesh):
    fine_mesh = Mesh(mesh.devices.reshape(RING_Y, DEPTH_Z, CORES, RING_X), AXES)
    placed = (
        P(AXES, None),
        P(None, AXES),
        P(TILE, "x", None, None),
        P(TILE),
        P(),
        P(),
        P(AXES, None),
    )
    return jax.shard_map(
        shards,
        mesh=fine_mesh,
        in_specs=placed,
        out_specs=(P(AXES, None), P(), P()),
        check_vma=False,
    )
```

```python
import jax
import jax.numpy as jnp
from jax import lax
from jax.experimental import pallas as pl
from jax.experimental.pallas import tpu as pltpu
from jax.sharding import Mesh, PartitionSpec as P

RING_Y, DEPTH_Z, CORES, RING_X = 4, 8, 2, 4
AXES = ("y", "z", "core", "x")
TILE = ("y", "z", "core")
UNROLL = 32
GRID_W, GRID_H = 8, 4


def device_index(place):
    tile = (place[0] * DEPTH_Z + place[1]) * CORES + place[2]
    return tile * RING_X + place[3]


def partner_pairs(partner):
    pairs = []
    for y in range(RING_Y):
        for z in range(DEPTH_Z):
            for core in range(CORES):
                for x in range(RING_X):
                    place = (y, z, core, x)
                    pairs.append((device_index(place), device_index(partner(*place))))
    return pairs


def send(value, partner):
    return lax.ppermute(value, AXES, partner_pairs(partner))


def across_core(y, z, core, x):
    return (y, z, 1 - core, x)


def square(step, hop):
    def partner(y, z, core, x):
        return (y ^ (hop if step & 2 else 0), z, core, x ^ (hop if step & 1 else 0))

    return partner


def first_ring(step):
    return lambda y, z, core, x: square(step, 1 if core else 3)(y, z, core, x)


def second_ring(step):
    return lambda y, z, core, x: square(step, 3 if core else 1)(y, z, core, x)


def along_z(step):
    return lambda y, z, core, x: (y, z ^ step, core, x)


def narrow(value):
    return value.astype(jnp.bfloat16)


def wide(value):
    return value.astype(jnp.float32)


def pick(parts, digit):
    return lax.dynamic_index_in_dim(parts, digit, 0, keepdims=False)


def scatter_ring(parts, digit, ring, extra):
    rows = parts.shape[1]
    first = jnp.concatenate([pick(parts, digit ^ 1), extra], axis=0)
    first = send(first, ring(1))
    received = [first[:rows]] + [send(pick(parts, digit ^ step), ring(step)) for step in (2, 3)]
    total = wide(pick(parts, digit))
    for part in received:
        total = total + wide(part)
    return narrow(total), first[rows:]


def swap(first, second, flip):
    return jnp.where(flip, second, first), jnp.where(flip, first, second)


def gather_pair(part, digit, partner):
    other = send(part, partner)
    return jnp.stack(swap(part, other, digit == 1))


def gather_ring(part, digit, ring):
    parts = [part] + [send(part, ring(step)) for step in (1, 2, 3)]
    low, high = digit % 2 == 1, digit // 2 == 1
    first, second = swap(parts[0], parts[1], low)
    third, fourth = swap(parts[2], parts[3], low)
    first, third = swap(first, third, high)
    second, fourth = swap(second, fourth, high)
    return jnp.stack([first, second, third, fourth])


def sum_over_devices(mine, other, coarse):
    y, z, core, x = (lax.axis_index(name) for name in AXES)
    near_x, near_y = (x ^ (x >> 1)) & 1, (y ^ (y >> 1)) & 1
    far_x, far_y = x >> 1, y >> 1
    near, far = near_x + 2 * near_y, far_x + 2 * far_y
    ring_one = jnp.where(core == 0, far, near)
    ring_two = jnp.where(core == 0, near, far)
    rows, lanes = mine.shape[0] // (RING_X * RING_Y), mine.shape[1]
    part = narrow(wide(mine) + wide(send(other, across_core)))
    hop_one, hop_two = jnp.where(core == 0, 3, 1), jnp.where(core == 0, 1, 3)
    quarters = coarse.reshape(RING_X, coarse.shape[0] // RING_X, lanes)
    extra = jnp.concatenate([pick(quarters, x ^ hop_one), pick(quarters, x ^ 2)], axis=0)
    part, extra = scatter_ring(part.reshape(4, 4 * rows, lanes), ring_one, first_ring, extra)
    quarter = quarters.shape[1]
    kept = wide(pick(quarters, x)) + wide(extra[:quarter])
    passed = narrow(wide(pick(quarters, x ^ hop_two)) + wide(extra[quarter:]))
    part, extra = scatter_ring(part.reshape(4, rows, lanes), ring_two, second_ring, passed)
    halves = narrow(kept + wide(extra)).reshape(2, quarter // 2, lanes)
    coarse_out = jnp.concatenate([halves[0], halves[1]], axis=1)
    for step in (1, 2, 7):
        part = narrow(wide(part) + wide(send(part, along_z(step))))
    part = gather_ring(part, ring_two, second_ring).reshape(RING_Y * rows, lanes)
    part = gather_ring(part, ring_one, first_ring).reshape(RING_X * RING_Y * rows, lanes)
    return wide(gather_pair(part, core, across_core)).reshape(-1, lanes), coarse_out


def ring_x(step):
    return lambda y, z, core, x: (y, z, core, x ^ step)


def share_over_x(value):
    return [value] + [send(value, ring_x(step)) for step in (1, 2, 3)]


def part_copies(parts, target, sems, first):
    x = lax.axis_index("x")
    rows = parts[0].shape[0]
    copies = []
    for step, part in enumerate(parts):
        place = target.at[pl.ds(pl.multiple_of((x ^ step) * rows, rows), rows)]
        copies.append(pltpu.make_async_copy(part, place, sems.at[first + step]))
    return copies


def copy_rows(table, target, picks, first, count):
    for start in range(0, count, UNROLL):
        places = range(start, min(start + UNROLL, count))
        rows = [table[pl.ds(picks[first + at], 1), :] for at in places]
        for at, row in zip(places, rows):
            target[at : at + 1, :] = row


def copy_pairs(table, target, words, first, count):
    half = count // 2
    for start in range(0, half, UNROLL // 2):
        rows = []
        for at in range(start, start + UNROLL // 2):
            word = words[first + at]
            rows.append((at, table[pl.ds(word & 0xFFFF, 1), :]))
            rows.append((half + at, table[pl.ds(lax.shift_right_logical(word, 16), 1), :]))
        for at, row in rows:
            target[at : at + 1, :] = row


def matmul(left, right, left_dim=1, right_dim=0):
    return lax.dot_general(
        left, right, (((left_dim,), (right_dim,)), ((), ())), preferred_element_type=jnp.float32
    )


def pick_halo(lists, part0, part1, part2, part3, out, tile_feats, table, stage, sems):
    tile_rows, channels = tile_feats.shape
    slots = stage.shape[0]
    copies = part_copies((part0, part1, part2, part3), tile_feats, sems, 0)
    for copy in copies:
        copy.start()
    table[pl.ds(tile_rows, 8), :] = jnp.zeros((8, channels), jnp.float32)
    out[...] = jnp.zeros_like(out)
    y, z, core = (lax.axis_index(name) for name in TILE)
    own = (y * DEPTH_Z + z) * CORES + core
    for copy in copies:
        copy.wait()
    table[pl.ds(0, tile_rows), :] = tile_feats[...].astype(jnp.float32)
    planes, lines = RING_X * RING_Y * DEPTH_Z * CORES // (RING_X * GRID_W * GRID_H), GRID_H

    def body(at, carry):
        line = own % (GRID_W * GRID_H) // GRID_W + at // 3 % 3 - 1
        column = own % GRID_W + at % 3 - 1
        inside = (line >= 0) & (line < lines) & (column >= 0) & (column < GRID_W)
        tile = (at // 9 % planes * GRID_H + line) * GRID_W + column
        tile = jnp.where(inside, tile, own)
        first = pl.multiple_of(tile * slots, slots)
        copy_rows(table, stage, lists, first, slots)
        out[pl.ds(first, slots), :] = stage[...].astype(jnp.bfloat16)
        return carry

    lax.fori_loop(0, 9 * planes, body, 0)


def grad_kernel(
    grad0, grad1, grad2, grad3, down_weight, link_column, parent_out, hidden_out, tile_grad, sems
):
    copies = part_copies((grad0, grad1, grad2, grad3), tile_grad, sems, 0)
    for copy in copies:
        copy.start()
    octants = down_weight.shape[0]
    rows, channels = hidden_out.shape
    link = link_column[...]
    octant = link % octants
    columns = lax.broadcasted_iota(jnp.int32, (rows, tile_grad.shape[0]), 1)
    at_parent = ((link // octants) == columns).astype(jnp.bfloat16)
    for copy in copies:
        copy.wait()
    parent_grad = matmul(at_parent, tile_grad[...]).astype(jnp.bfloat16)
    hidden_grad = jnp.zeros((rows, channels), jnp.float32)
    for o in range(octants):
        back = matmul(parent_grad, down_weight[o], 1, 1)
        hidden_grad += jnp.where(octant == o, back, 0.0)
    parent_out[...] = parent_grad
    hidden_out[...] = hidden_grad


def step_kernel(
    kernel_map, part0, part1, part2, part3, incoming, conv_hbm, down_hbm, parent_hbm, back_hbm,
    link_column, link_row,
    coarse, mine, other,
    tile_feats, table, stage, gathered, pre_act, conv_weight, down_weight, parent_grad, back_grad, sems,
):
    rows, channels = part0.shape
    offsets = conv_weight.shape[0]
    octants, _, out_channels = down_weight.shape
    tile_rows, halo_rows = tile_feats.shape[0], incoming.shape[0]
    coarse_tile = coarse.shape[0] * channels // out_channels
    feats = part_copies((part0, part1, part2, part3), tile_feats, sems, 0)
    conv = pltpu.make_async_copy(conv_hbm, conv_weight, sems.at[4])
    late = [
        pltpu.make_async_copy(down_hbm, down_weight, sems.at[5]),
        pltpu.make_async_copy(parent_hbm, parent_grad, sems.at[6]),
        pltpu.make_async_copy(back_hbm, back_grad, sems.at[7]),
    ]
    for copy in feats + [conv] + late:
        copy.start()
    pre_act[...] = jnp.zeros_like(pre_act)
    table[pl.ds(tile_rows + halo_rows, 8), :] = jnp.zeros((8, channels), jnp.float32)
    table[pl.ds(tile_rows, halo_rows), :] = incoming[...].astype(jnp.float32)
    for copy in feats:
        copy.wait()
    table[pl.ds(0, tile_rows), :] = tile_feats[...].astype(jnp.float32)
    middle = offsets // 2
    own = pl.multiple_of(lax.axis_index("x") * rows, rows)
    gathered[middle] = tile_feats[pl.ds(own, rows), :]
    conv.wait()

    def forward(at, previous):
        offset = at + (at >= middle).astype(jnp.int32)
        pre_act[...] += matmul(gathered[previous], conv_weight[previous])
        copy_pairs(table, stage, kernel_map, offset * (rows // 2), rows)
        gathered[offset] = stage[...].astype(jnp.bfloat16)
        return offset

    last = lax.fori_loop(0, offsets - 1, forward, jnp.int32(middle))
    for copy in late:
        copy.wait()
    act = pre_act[...] + matmul(gathered[last], conv_weight[last])
    gate = 1.0 / (1.0 + jnp.exp(-act))
    hidden_wide = act * gate
    hidden = hidden_wide.astype(jnp.bfloat16)
    hidden_turned = hidden_wide.T.astype(jnp.bfloat16)
    pre_grad = back_grad[...] * gate * (1.0 + act * (1.0 - gate))
    pre_grad_turned = pre_grad.T.astype(jnp.bfloat16)
    octant = link_column[...] % octants
    link_turned = link_row[...]
    octant_turned = link_turned % octants
    own_term = jnp.zeros((rows, out_channels), jnp.float32)
    for o in range(octants):
        only = jnp.where(octant == o, hidden, jnp.zeros_like(hidden))
        own_term += matmul(only, down_weight[o])
    from_row = (link_turned // octants) == lax.broadcasted_iota(jnp.int32, (coarse_tile, rows), 0)
    from_row = from_row.astype(jnp.bfloat16)
    high = own_term.astype(jnp.bfloat16)
    low = (own_term - high.astype(jnp.float32)).astype(jnp.bfloat16)
    coarse_sums = (matmul(from_row, high) + matmul(from_row, low)).astype(jnp.bfloat16)
    quarter = coarse_tile // RING_X
    for at in range(2 * RING_X):
        block = coarse_sums[at // 2 * quarter : (at // 2 + 1) * quarter]
        block = block[:, at % 2 * channels : (at % 2 + 1) * channels]
        coarse[pl.ds(at * quarter, quarter), :] = block

    half_blocks = mine.shape[0] // channels
    down_first = offsets - half_blocks

    def fill(first, second):
        def backward(target, start):
            def body(at, carry):
                turned = matmul(pre_grad_turned, gathered[start + at])
                place = pl.ds(pl.multiple_of(at * channels, channels), channels)
                target[place, :] = turned.T.astype(jnp.bfloat16)
                return carry

            return body

        lax.fori_loop(0, half_blocks, backward(first, 0), 0, unroll=True)
        lax.fori_loop(0, down_first, backward(second, half_blocks), 0, unroll=True)
        for o in range(octants):
            only = jnp.where(octant_turned == o, hidden_turned, jnp.zeros_like(hidden_turned))
            product = matmul(only, parent_grad[...]).astype(jnp.bfloat16)
            left, right = (down_first + o) * channels, (down_first + octants + o) * channels
            second[pl.ds(left, channels), :] = product[:, :channels]
            second[pl.ds(right, channels), :] = product[:, channels:]
        used = (down_first + 2 * octants) * channels
        second[pl.ds(used, second.shape[0] - used), :] = jnp.zeros(
            (second.shape[0] - used, channels), jnp.bfloat16
        )

    core = lax.axis_index("core")

    @pl.when(core == 0)
    def _():
        fill(mine, other)

    @pl.when(core == 1)
    def _():
        fill(other, mine)


def shards(features, kernel_map, send_lists, fine_to_coarse, conv_weight, down_weight, coarse_grad):
    rows, channels = features.shape
    tiles, slots = send_lists.shape[2:]
    offsets = kernel_map.shape[0]
    octants, _, out_channels = down_weight.shape
    tile_rows, halo_rows = RING_X * rows, tiles * slots
    coarse_rows = coarse_grad.shape[0]
    coarse_tile = RING_X * coarse_rows
    smem, vmem = pl.BlockSpec(memory_space=pltpu.SMEM), pl.BlockSpec(memory_space=pltpu.VMEM)
    anywhere = pl.BlockSpec(memory_space=pltpu.HBM)
    parts = share_over_x(features)
    outgoing = pl.pallas_call(
        pick_halo,
        out_shape=jax.ShapeDtypeStruct((halo_rows, channels), jnp.bfloat16),
        in_specs=[smem] + [anywhere] * 4,
        out_specs=vmem,
        scratch_shapes=[
            pltpu.VMEM((tile_rows, channels), jnp.bfloat16),
            pltpu.VMEM((tile_rows + 8, channels), jnp.float32),
            pltpu.VMEM((slots, channels), jnp.float32),
            pltpu.SemaphoreType.DMA((4,)),
        ],
        compiler_params=pltpu.CompilerParams(vmem_limit_bytes=56 << 20),
        name="pick_halo",
    )(send_lists.reshape(halo_rows), *parts)
    later_grad, outgoing = lax.optimization_barrier((coarse_grad, outgoing))
    incoming = lax.all_to_all(
        outgoing.reshape(tiles, slots, channels), TILE, split_axis=0, concat_axis=0, tiled=True
    )
    grads = share_over_x(later_grad)
    x = lax.axis_index("x")
    link = lax.dynamic_slice_in_dim(fine_to_coarse, x * rows, rows)
    used = offsets * channels + 2 * octants * channels
    total = used + (-used % 512)
    link_column, link_row = link.reshape(rows, 1), link.reshape(1, rows)
    parent_grad, back_grad = pl.pallas_call(
        grad_kernel,
        out_shape=(
            jax.ShapeDtypeStruct((rows, out_channels), jnp.bfloat16),
            jax.ShapeDtypeStruct((rows, channels), jnp.float32),
        ),
        in_specs=[anywhere] * 4 + [vmem] * 2,
        out_specs=(vmem, vmem),
        scratch_shapes=[
            pltpu.VMEM((coarse_tile, out_channels), jnp.bfloat16),
            pltpu.SemaphoreType.DMA((4,)),
        ],
        compiler_params=pltpu.CompilerParams(vmem_limit_bytes=56 << 20),
        name="coarse_back",
    )(*grads, down_weight, link_column)
    half = total // CORES
    map_pairs = kernel_map[:, : rows // 2] | (kernel_map[:, rows // 2 :] << 16)
    map_pairs = map_pairs.reshape(offsets * rows // 2)
    coarse, mine, other = pl.pallas_call(
        step_kernel,
        out_shape=(
            jax.ShapeDtypeStruct((coarse_tile * out_channels // channels, channels), jnp.bfloat16),
            jax.ShapeDtypeStruct((half, channels), jnp.bfloat16),
            jax.ShapeDtypeStruct((half, channels), jnp.bfloat16),
        ),
        in_specs=[smem] + [anywhere] * 4 + [vmem] + [anywhere] * 4 + [vmem] * 2,
        out_specs=(vmem, vmem, vmem),
        scratch_shapes=[
            pltpu.VMEM((tile_rows, channels), jnp.bfloat16),
            pltpu.VMEM((tile_rows + halo_rows + 8, channels), jnp.float32),
            pltpu.VMEM((rows, channels), jnp.float32),
            pltpu.VMEM((offsets, rows, channels), jnp.bfloat16),
            pltpu.VMEM((rows, channels), jnp.float32),
            pltpu.VMEM(conv_weight.shape, jnp.bfloat16),
            pltpu.VMEM(down_weight.shape, jnp.bfloat16),
            pltpu.VMEM((rows, out_channels), jnp.bfloat16),
            pltpu.VMEM((rows, channels), jnp.float32),
            pltpu.SemaphoreType.DMA((8,)),
        ],
        compiler_params=pltpu.CompilerParams(vmem_limit_bytes=56 << 20),
        name="step",
    )(
        map_pairs, *parts, incoming.reshape(halo_rows, channels),
        conv_weight, down_weight, parent_grad, back_grad, link_column, link_row,
    )
    sums, coarse_out = sum_over_devices(mine, other, coarse)
    conv_grad = sums[: offsets * channels].reshape(offsets, channels, channels)
    down_sums = sums[offsets * channels : used]
    half = octants * channels
    down_grad = jnp.concatenate([down_sums[:half], down_sums[half:]], axis=1)
    down_grad = down_grad.reshape(octants, channels, out_channels)
    return (coarse_out, conv_grad, down_grad)


def solution(mesh):
    fine_mesh = Mesh(mesh.devices.reshape(RING_Y, DEPTH_Z, CORES, RING_X), AXES)
    placed = (
        P(AXES, None),
        P(None, AXES),
        P(TILE, "x", None, None),
        P(TILE),
        P(),
        P(),
        P(AXES, None),
    )
    return jax.shard_map(
        shards,
        mesh=fine_mesh,
        in_specs=placed,
        out_specs=(P(AXES, None), P(), P()),
        check_vma=False,
    )
```
